32 devices in a mesh: seq: 2 (over core), ctx: 8 (over z, y), head: 2 (over x).
Axes of the slice: x: 2, y: 2, z: 4, core: 2. Of those that a mesh axis runs over, the one named last changes fastest.
Arguments:
- queries: bfloat16 [2048, 8, 128], P(('seq', 'ctx'), 'head'), parts along dimension 0, may hold values from -8 to 8
- key_rows: bfloat16 [2048, 128], P(('seq', 'ctx')), parts along dimension 0, may hold values from -8 to 8
- value_rows: bfloat16 [2048, 128], P(('seq', 'ctx')), parts along dimension 0, may hold values from -6 to 6
- out_grad: bfloat16 [2048, 8, 128], P(('seq', 'ctx'), 'head'), parts along dimension 0, may hold values from -6 to 6
- doc_lengths: int32 [16], P('seq'), parts along dimension 0, may hold values from 1 to 256, 1024 in all
- balance: int32 [2048], P('seq'), parts along dimension 0, may hold values from 0 to 1023, as said below
Outputs:
- attended: bfloat16 [2048, 8, 128], P(('seq', 'ctx'), 'head'), parts along dimension 0
- query_grad: bfloat16 [2048, 8, 128], P(('seq', 'ctx'), 'head'), parts along dimension 0
- key_grad: bfloat16 [2048, 128], P(('seq', 'ctx')), parts along dimension 0
- value_grad: bfloat16 [2048, 128], P(('seq', 'ctx')), parts along dimension 0
The draws below stay inside these ranges and needn't reach their ends.
There are 2 independent parts, one for each index of `seq`. The reference program is written for one: setup_inputs(seed, part) draws one part's arguments, and reference() takes and returns one part's arrays. A program takes and returns all parts, laid end to end along the dimension named above; each array names one. Nothing has to cross between parts.
Inputs may be any that keep to these rules, and one draw needn't show every extreme that they name: `doc_lengths`: the lengths sum to 1024 and the longest is exactly 256. `balance`: A permutation of the positions that moves aligned runs of 64 positions whole and in order.
All inputs are finite; a program needn't handle non-finite values.
Results may differ from the reference program's by a relative error of at most 0.034.
Values may be sent and summed in bfloat16 or wider, within the bound.
No kernel may reach another device: no remote copies, remote signals or barrier semaphores. Data moves between devices by JAX's collectives and lax.ppermute only.
A program may use at most 64 MiB of HBM per device.

```python
import math
import jax
import jax.numpy as jnp
import numpy as np
from jax import lax

HEADS = 8
DH = 128
SEQ = 1024
HALF = 64
SPANS = 16
DOCS = 8
MOST_DOC = 256


def draw_queries(key, part):
    values_now = jnp.clip(jax.random.normal(jax.random.fold_in(key, 11), (SEQ, HEADS, DH), jnp.float32), -6.0, 6.0)
    return values_now.astype(jnp.bfloat16)


def draw_key_rows(key, part):
    values_now = jnp.clip(jax.random.normal(jax.random.fold_in(key, 13), (SEQ, DH), jnp.float32), -6.0, 6.0)
    return values_now.astype(jnp.bfloat16)


def draw_balance(key, part):
    span_order = jax.random.permutation(jax.random.fold_in(key, 17), SPANS).astype(jnp.int32)
    offsets = jnp.arange(HALF, dtype=jnp.int32)
    return (span_order[:, None] * HALF + offsets[None, :]).reshape(-1).astype(jnp.int32)


def level_of(own_key, shape, shards, smallest, top_value):
    def one(axis_at, blocks):
        draws = jax.random.uniform(jax.random.fold_in(jax.random.fold_in(own_key, 6), axis_at), (blocks,), jnp.float32, smallest / len(shards), top_value / len(shards))
        return jnp.repeat(jnp.exp(draws), shape[axis_at] // blocks).reshape((-1,) + (1,) * (len(shape) - axis_at - 1))

    loudness = one(*shards[0])
    for cut in shards[1:]:
        loudness = loudness * one(*cut)
    return loudness


def length_profile(count, total, reach, lean):
    portions = [(1 << 20) // math.isqrt(rank ** lean) + 1 for rank in range(2, count + 1)]
    spare, holding = total - reach - (count - 1), [1] * (count - 1)
    while spare > 0:
        candidates = [i for i in range(count - 1) if holding[i] < reach]
        mass, left = sum([portions[i] for i in candidates]), spare
        for i in candidates:
            more = min(reach - holding[i], max(1, left * portions[i] // mass), spare)
            holding[i] = holding[i] + more
            spare = spare - more
    return np.array([reach] + holding)


def uneven(own_key, number_of, total, reach, lean):
    if number_of == 2:
        one = jax.random.randint(own_key, (), max(1, total - reach), min(reach, total - 1) + 1)
        return jnp.stack([one, total - one])
    sizes = jnp.asarray(length_profile(number_of, total, reach, lean), jnp.int32)
    couples = (number_of - 1) // 2
    donor, taker = sizes[1:1 + 2 * couples:2], sizes[2:2 + 2 * couples:2]
    slack = jnp.minimum(donor - 1, reach - taker)
    moved = jax.random.randint(jax.random.fold_in(own_key, 1), (couples,), 0, 1 << 20) % (slack + 1)
    sizes = sizes.at[1:1 + 2 * couples:2].set(donor - moved).at[2:2 + 2 * couples:2].set(taker + moved)
    return sizes[jax.random.permutation(jax.random.fold_in(own_key, 2), number_of)]


def gaussian(rng, shape, deviation, bound, split=(), kind=jnp.bfloat16):
    array = deviation * jax.random.normal(rng, shape, jnp.float32)
    if split:
        array = array * level_of(rng, shape, split, -0.22, 0.18)
    return jnp.clip(array, -bound, bound).astype(kind)


def setup_inputs(seed: int = 0, part: int = 0) -> dict:
    splits = jax.random.split(jax.random.key(seed), 7)
    part_splits = jax.random.split(jax.random.fold_in(splits[6], part), 7)
    queries = draw_queries(jax.random.fold_in(jax.random.fold_in(splits[6], part), 71), part)
    key_rows = draw_key_rows(jax.random.fold_in(jax.random.fold_in(splits[6], part), 71), part)
    value_rows = gaussian(part_splits[2], (SEQ, DH), 1.0, 6.0, ((0, 8),))
    out_grad = gaussian(part_splits[3], (SEQ, HEADS, DH), 1.0, 6.0, ((0, 8), (1, 2)))
    doc_lengths = uneven(part_splits[4], DOCS, SEQ, MOST_DOC, 2).astype(jnp.int32)
    balance = draw_balance(jax.random.fold_in(jax.random.fold_in(splits[6], part), 71), part)
    return {"queries": queries, "key_rows": key_rows, "value_rows": value_rows, "out_grad": out_grad, "doc_lengths": doc_lengths, "balance": balance}


NEGATIVE = -1e+30

def rounded(values):
    return lax.optimization_barrier(values.astype(jnp.bfloat16)).astype(jnp.float32)

def document_of(positions, doc_lengths):
    doc_ends = jnp.cumsum(doc_lengths).astype(jnp.int32)
    return lax.optimization_barrier(jnp.sum((positions[:, None] >= doc_ends[None, :]).astype(jnp.int32), axis=1)).astype(jnp.int32)

def reference(queries, key_rows, value_rows, out_grad, doc_lengths, balance):
    scaling = 1.0 / math.sqrt(DH)
    docs_all = document_of(balance, doc_lengths)
    block_len = min(512, SEQ)
    block_count = SEQ // block_len
    keys_f = key_rows.astype(jnp.float32)
    values_f = value_rows.astype(jnp.float32)
    query_blocks = queries.reshape(block_count, block_len, HEADS, DH)
    grad_blocks = out_grad.reshape(block_count, block_len, HEADS, DH)
    pos_blocks = balance.reshape(block_count, block_len)
    doc_blocks = docs_all.reshape(block_count, block_len)

    def step_block(state_now, inputs_now):
        key_acc, value_acc = state_now
        query_blk, grad_blk, query_pos, query_doc = inputs_now
        visible_pairs = (docs_all[None, :] == query_doc[:, None]) & (balance[None, :] <= query_pos[:, None])
        allowed = visible_pairs[:, None, :]
        query_f = query_blk.astype(jnp.float32)
        grad_f = grad_blk.astype(jnp.float32)
        scores = jnp.einsum('qhd,kd->qhk', query_f, keys_f) * scaling
        scores = jnp.where(allowed, scores, NEGATIVE)
        row_max = lax.optimization_barrier(jnp.max(scores, axis=2))
        raw_weights = jnp.where(allowed, jnp.exp(scores - row_max[:, :, None]), 0.0)
        weight_sum = lax.optimization_barrier(jnp.sum(raw_weights, axis=2))
        attended_blk = (jnp.einsum('qhk,kd->qhd', rounded(raw_weights), values_f) / weight_sum[:, :, None]).astype(jnp.bfloat16)
        log_total = row_max + jnp.log(weight_sum)
        weights = jnp.where(allowed, jnp.exp(scores - log_total[:, :, None]), 0.0)
        row_inner = lax.optimization_barrier(jnp.sum(grad_f * attended_blk.astype(jnp.float32), axis=2))
        grad_weights = jnp.einsum('qhd,kd->qhk', grad_f, values_f)
        grad_scores = rounded(weights * (grad_weights - row_inner[:, :, None]))
        query_grad_blk = (jnp.einsum('qhk,kd->qhd', grad_scores, keys_f) * scaling).astype(jnp.bfloat16)
        key_acc = key_acc + jnp.einsum('qhk,qhd->kd', grad_scores, query_f) * scaling
        value_acc = value_acc + jnp.einsum('qhk,qhd->kd', rounded(weights), grad_f)
        return ((key_acc, value_acc), (attended_blk, query_grad_blk))
    start_state = (jnp.zeros((SEQ, DH), jnp.float32), jnp.zeros((SEQ, DH), jnp.float32))
    final_state, outputs = lax.scan(step_block, start_state, (query_blocks, grad_blocks, pos_blocks, doc_blocks))
    attended = outputs[0].reshape(SEQ, HEADS, DH)
    query_grad = outputs[1].reshape(SEQ, HEADS, DH)
    return (attended, query_grad, final_state[0].astype(jnp.bfloat16), final_state[1].astype(jnp.bfloat16))
```

```python
import functools
import math

import jax
import jax.numpy as jnp
from jax import lax
from jax.experimental import pallas as pl
from jax.experimental.pallas import tpu as pltpu
from jax.sharding import PartitionSpec as P

NEGATIVE = -1e30
RUN = 64
LONGEST_SHARE = 4

ANY = pl.BlockSpec(memory_space=pl.ANY)
SMEM = pl.BlockSpec(memory_space=pltpu.SMEM)


def contract(a, b, dim_a, dim_b):
    return lax.dot_general(
        a, b, (((dim_a,), (dim_b,)), ((), ())), preferred_element_type=jnp.float32
    )


def attention_kernel(n_ctx, heads, place, balance, doc_lengths, q_in, g_in, *refs):
    blocks = refs[:n_ctx]
    att_out, qg_out = refs[n_ctx : n_ctx + 2]
    terms_out = refs[n_ctx + 2 : 2 * n_ctx + 2]
    scratch = refs[2 * n_ctx + 2 :]
    q_all, g_all, kv_all, window, terms, att_buf, qg_buf, bf_buf, f32_buf, slot_of, in_sem, out_sem = scratch
    me = place[0]
    tok_rows = blocks[0].shape[0]
    width = blocks[0].shape[1] // 2
    seq_total = kv_all.shape[0]
    runs_here = tok_rows // RUN
    reach = window.shape[1] // RUN
    run_rows = RUN * heads
    docs = doc_lengths.shape[0]
    scaling = 1.0 / math.sqrt(width)

    copies = [pltpu.make_async_copy(q_in, q_all, in_sem.at[0]), pltpu.make_async_copy(g_in, g_all, in_sem.at[1])]
    for k in range(n_ctx):
        owner = lax.bitwise_xor(me, k)
        rows = pl.ds(pl.multiple_of(owner * tok_rows, tok_rows), tok_rows)
        copies.append(pltpu.make_async_copy(blocks[k], kv_all.at[rows], in_sem.at[2 + k]))
    for copy in copies:
        copy.start()

    def note(s, carry):
        slot_of[lax.shift_right_logical(balance[s * RUN], 6)] = s
        return carry

    lax.fori_loop(0, seq_total // RUN, note, 0, unroll=seq_total // RUN <= 16)
    terms[...] = jnp.zeros_like(terms)
    for copy in copies:
        copy.wait()

    for r in range(runs_here):
        place_run = lax.shift_right_logical(balance[me * tok_rows + r * RUN], 6)
        slots = []
        for j in range(reach):
            slot = slot_of[jnp.maximum(place_run - (reach - 1) + j, 0)]
            rows = pl.ds(pl.multiple_of(slot * RUN, RUN), RUN)
            slots.append(rows)
            window[r, j * RUN : (j + 1) * RUN, :] = kv_all[rows, :]
        keys = window[r, :, :width]
        values = window[r, :, width:]
        q_rows = q_all[r * run_rows : (r + 1) * run_rows, :]
        g_rows = g_all[r * run_rows : (r + 1) * run_rows, :]

        lane = lax.broadcasted_iota(jnp.int32, (1, run_rows), 1)
        q_pos = place_run * RUN + lax.div(lane, heads)
        doc_start = jnp.zeros_like(q_pos)
        doc_end = jnp.int32(0)
        for d in range(docs):
            doc_end = doc_end + doc_lengths[d]
            doc_start = jnp.where(doc_end <= q_pos, doc_end, doc_start)
        k_pos = (place_run - (reach - 1)) * RUN + lax.broadcasted_iota(jnp.int32, (reach * RUN, run_rows), 0)
        visible = (k_pos >= doc_start) & (k_pos <= q_pos)

        scores = jnp.where(visible, contract(keys, q_rows, 1, 1), NEGATIVE)
        top = jnp.max(scores, axis=0, keepdims=True)
        raw = jnp.exp((scores - top) * scaling)
        one_over = 1.0 / jnp.sum(raw, axis=0, keepdims=True)
        attended = contract(values, raw.astype(jnp.bfloat16), 0, 0) * one_over
        att_buf[r * run_rows : (r + 1) * run_rows, :] = attended.T.astype(jnp.bfloat16)

        weights = raw * one_over
        grad_weights = contract(values, g_rows, 1, 1)
        row_inner = jnp.sum(weights * grad_weights, axis=0, keepdims=True)
        grad_scores = (weights * (grad_weights - row_inner)).astype(jnp.bfloat16)
        value_part = contract(weights.astype(jnp.bfloat16), g_rows, 1, 0)
        key_part = contract(grad_scores, q_rows, 1, 0) * scaling
        query_part = contract(keys, grad_scores, 0, 0) * scaling
        qg_buf[r * run_rows : (r + 1) * run_rows, :] = query_part.T.astype(jnp.bfloat16)
        for j in range(reach):
            part = slice(j * RUN, (j + 1) * RUN)
            terms[slots[j], :width] += key_part[part, :]
            terms[slots[j], width:] += value_part[part, :]

    out_copies = []
    for k in range(n_ctx):
        owner = lax.bitwise_xor(me, k)
        rows = pl.ds(pl.multiple_of(owner * tok_rows, tok_rows), tok_rows)
        if k % 2:
            bf_buf[k // 2] = terms[rows, :].astype(jnp.bfloat16)
            out_copies.append(pltpu.make_async_copy(bf_buf.at[k // 2], terms_out[k], out_sem.at[k]))
        else:
            out_copies.append(pltpu.make_async_copy(terms.at[rows], terms_out[k], out_sem.at[k]))
        out_copies[-1].start()
    out_copies.append(pltpu.make_async_copy(att_buf, att_out, out_sem.at[n_ctx]))
    out_copies.append(pltpu.make_async_copy(qg_buf, qg_out, out_sem.at[n_ctx + 1]))
    out_copies[-2].start()
    out_copies[-1].start()
    for copy in out_copies:
        copy.wait()


def attention(place, balance, doc_lengths, q_rows, g_rows, blocks, heads):
    n_ctx = len(blocks)
    tok_rows, both = blocks[0].shape
    width = both // 2
    seq_total = balance.shape[0]
    reach = seq_total // LONGEST_SHARE // RUN + 1
    rows = q_rows.shape[0]
    outs = [jax.ShapeDtypeStruct((rows, width), jnp.bfloat16)] * 2
    for k in range(n_ctx):
        outs.append(jax.ShapeDtypeStruct((tok_rows, both), jnp.bfloat16 if k % 2 else jnp.float32))
    return pl.pallas_call(
        functools.partial(attention_kernel, n_ctx, heads),
        out_shape=outs,
        in_specs=[SMEM] * 3 + [ANY] * (2 + n_ctx),
        out_specs=[ANY] * len(outs),
        scratch_shapes=[
            pltpu.VMEM((rows, width), jnp.bfloat16),
            pltpu.VMEM((rows, width), jnp.bfloat16),
            pltpu.VMEM((seq_total, both), jnp.bfloat16),
            pltpu.VMEM((tok_rows // RUN, reach * RUN, both), jnp.bfloat16),
            pltpu.VMEM((seq_total, both), jnp.float32),
            pltpu.VMEM((rows, width), jnp.bfloat16),
            pltpu.VMEM((rows, width), jnp.bfloat16),
            pltpu.VMEM((n_ctx // 2, tok_rows, both), jnp.bfloat16),
            pltpu.VMEM((8, 128), jnp.float32),
            pltpu.SMEM((seq_total // RUN,), jnp.int32),
            pltpu.SemaphoreType.DMA((2 + n_ctx,)),
            pltpu.SemaphoreType.DMA((2 + n_ctx,)),
        ],
        compiler_params=pltpu.CompilerParams(
            vmem_limit_bytes=(16 << 20) if seq_total <= 1024 else (56 << 20)
        ),
    )(place, balance, doc_lengths, q_rows, g_rows, *blocks)


def body(n_ctx, n_head, queries, key_rows, value_rows, out_grad, doc_lengths, balance):
    tok_rows, heads, width = queries.shape

    def swap(array, k):
        return lax.ppermute(array, "ctx", [(i, i ^ k) for i in range(n_ctx)])

    mine = jnp.concatenate([key_rows, value_rows], axis=1)
    blocks = {0: mine}
    far_first = list(range(n_ctx - 2, 0, -2))
    for k in far_first:
        blocks[k] = swap(mine, k)
    blocks[1] = swap(mine, 1)
    for k in reversed(far_first):
        blocks[k + 1] = swap(blocks[k], 1)

    place = lax.axis_index("ctx").astype(jnp.int32).reshape(1)
    attended, query_grad, *terms = attention(
        place,
        balance,
        doc_lengths,
        queries.reshape(tok_rows * heads, width),
        out_grad.reshape(tok_rows * heads, width),
        [blocks[k] for k in range(n_ctx)],
        heads,
    )

    arrived = {}
    for k in far_first:
        arrived[k] = swap(terms[k + 1], 1)
    arrived[0] = swap(terms[1], 1)
    total = terms[0] + arrived[0].astype(jnp.float32)
    for k in far_first:
        pair = (terms[k] + arrived[k].astype(jnp.float32)).astype(jnp.bfloat16)
        total = total + swap(pair, k).astype(jnp.float32)
    mine = total.astype(jnp.bfloat16)
    other = lax.ppermute(mine, "head", [(i, (i + 1) % n_head) for i in range(n_head)])
    combined = (mine.astype(jnp.float32) + other.astype(jnp.float32)).astype(jnp.bfloat16)
    return (
        attended.reshape(tok_rows, heads, width),
        query_grad.reshape(tok_rows, heads, width),
        combined[:, :width],
        combined[:, width:],
    )


def solution(mesh):
    return jax.shard_map(
        functools.partial(body, mesh.shape["ctx"], mesh.shape["head"]),
        mesh=mesh,
        in_specs=(
            P(("seq", "ctx"), "head", None),
            P(("seq", "ctx"), None),
            P(("seq", "ctx"), None),
            P(("seq", "ctx"), "head", None),
            P("seq"),
            P("seq"),
        ),
        out_specs=(
            P(("seq", "ctx"), "head", None),
            P(("seq", "ctx"), "head", None),
            P(("seq", "ctx"), None),
            P(("seq", "ctx"), None),
        ),
        check_vma=False,
    )
```

```python
import functools
import math

import jax
import jax.numpy as jnp
from jax import lax
from jax.experimental import pallas as pl
from jax.experimental.pallas import tpu as pltpu
from jax.sharding import PartitionSpec as P

NEGATIVE = -1e30
RUN = 64
LONGEST_SHARE = 4

ANY = pl.BlockSpec(memory_space=pl.ANY)
VMEM = pl.BlockSpec(memory_space=pltpu.VMEM)
HBM = pl.BlockSpec(memory_space=pltpu.HBM)
SMEM = pl.BlockSpec(memory_space=pltpu.SMEM)


def contract(a, b, dim_a, dim_b):
    return lax.dot_general(
        a, b, (((dim_a,), (dim_b,)), ((), ())), preferred_element_type=jnp.float32
    )


def limit(seq_total):
    return pltpu.CompilerParams(vmem_limit_bytes=(16 << 20) if seq_total <= 1024 else (56 << 20))


def goes_first_over_y(k):
    return k % 2 == 1 and k > 3


def pack_kernel(key_rows, value_rows, q_rows, g_rows, kv_out, qg_out, sems):
    tok_rows, rows = key_rows.shape[0], q_rows.shape[0]
    copies = [
        pltpu.make_async_copy(key_rows, kv_out.at[pl.ds(0, tok_rows)], sems.at[0]),
        pltpu.make_async_copy(value_rows, kv_out.at[pl.ds(tok_rows, tok_rows)], sems.at[1]),
        pltpu.make_async_copy(q_rows, qg_out.at[pl.ds(0, rows)], sems.at[2]),
        pltpu.make_async_copy(g_rows, qg_out.at[pl.ds(rows, rows)], sems.at[3]),
    ]
    for copy in copies:
        copy.start()
    for copy in copies:
        copy.wait()


def pack(key_rows, value_rows, q_rows, g_rows, seq_total):
    return pl.pallas_call(
        pack_kernel,
        out_shape=[
            jax.ShapeDtypeStruct((2 * key_rows.shape[0], key_rows.shape[1]), jnp.bfloat16),
            jax.ShapeDtypeStruct((2 * q_rows.shape[0], q_rows.shape[1]), jnp.bfloat16),
        ],
        in_specs=[ANY] * 4,
        out_specs=[ANY] * 2,
        scratch_shapes=[pltpu.SemaphoreType.DMA((4,))],
        compiler_params=limit(seq_total),
    )(*[pltpu.with_memory_space_constraint(a, pltpu.HBM) for a in (key_rows, value_rows, q_rows, g_rows)])


def table_size(runs_here, reach, docs):
    return -(-(2 + runs_here * (1 + reach) + docs) // 128) * 128


def table_kernel(runs_here, reach, place, balance, doc_lengths, after, table_out, table, slot_of, sem):
    runs = balance.shape[0] // RUN
    docs = doc_lengths.shape[0]

    def note(s, carry):
        slot_of[lax.shift_right_logical(balance[s * RUN], 6)] = s
        return carry

    lax.fori_loop(0, runs, note, 0, unroll=runs <= 16)
    table[0] = place[0]
    table[1] = place[1]
    for r in range(runs_here):
        at = 2 + r * (1 + reach)
        place_run = lax.shift_right_logical(balance[(place[0] * runs_here + r) * RUN], 6)
        table[at] = place_run
        for j in range(reach):
            table[at + 1 + j] = slot_of[jnp.maximum(place_run - (reach - 1) + j, 0)]
    end = jnp.int32(0)
    for d in range(docs):
        end = end + doc_lengths[d]
        table[2 + runs_here * (1 + reach) + d] = end
    copy = pltpu.make_async_copy(table, table_out, sem)
    copy.start()
    copy.wait()


def make_table(place, balance, doc_lengths, after, runs_here, reach):
    size = table_size(runs_here, reach, doc_lengths.shape[0])
    runs = balance.shape[0] // RUN
    return pl.pallas_call(
        functools.partial(table_kernel, runs_here, reach),
        out_shape=jax.ShapeDtypeStruct((size,), jnp.int32),
        in_specs=[SMEM] * 3 + [ANY],
        out_specs=ANY,
        scratch_shapes=[
            pltpu.SMEM((size,), jnp.int32),
            pltpu.SMEM((runs,), jnp.int32),
            pltpu.SemaphoreType.DMA,
        ],
        compiler_params=limit(balance.shape[0]),
    )(place, balance, doc_lengths, after)


def run_window(table, kv_all, key_win, value_win, r, reach, runs_here, tok_rows):
    at = 2 + r * (1 + reach)
    rows = []
    for j in range(reach):
        slot = table[at + 1 + j]
        row = lax.div(slot, runs_here) * (2 * tok_rows) + lax.rem(slot, runs_here) * RUN
        row = pl.multiple_of(row, RUN)
        rows.append(row)
        key_win[r, j * RUN : (j + 1) * RUN, :] = kv_all[pl.ds(row, RUN), :]
        value_win[r, j * RUN : (j + 1) * RUN, :] = kv_all[pl.ds(row + tok_rows, RUN), :]
    return rows


def weights_of(table, keys, q_rows, r, reach, runs_here, docs, heads):
    count = q_rows.shape[0]
    place_run = table[2 + r * (1 + reach)]
    scaling = math.log2(math.e) / math.sqrt(keys.shape[1])
    lane = lax.broadcasted_iota(jnp.int32, (1, count), 1)
    q_off = lax.div(lax.rem(lane, RUN * heads), heads)
    q_pos = place_run * RUN + q_off
    doc_start = jnp.zeros_like(q_pos)
    for d in range(docs):
        doc_end = table[2 + runs_here * (1 + reach) + d]
        doc_start = jnp.where(doc_end <= q_pos, doc_end, doc_start)
    doc_start = doc_start - (place_run - (reach - 1)) * RUN
    scores = contract(keys, q_rows, 1, 1)
    early = (reach - 1) * RUN
    k_early = lax.broadcasted_iota(jnp.int32, (early, count), 0)
    k_own = lax.broadcasted_iota(jnp.int32, (RUN, count), 0)
    scores = jnp.concatenate(
        [
            jnp.where(k_early >= doc_start, scores[:early], NEGATIVE),
            jnp.where((k_own + early >= doc_start) & (k_own <= q_off), scores[early:], NEGATIVE),
        ],
        axis=0,
    )
    top = jnp.max(scores, axis=0, keepdims=True)
    raw = jnp.exp2((scores - top) * scaling)
    return raw, 1.0 / jnp.sum(raw, axis=0, keepdims=True)


def score_gradients(raw, one_over, values, g_rows):
    weights = raw * one_over
    grad_weights = contract(values, g_rows, 1, 1)
    row_inner = jnp.sum(weights * grad_weights, axis=0, keepdims=True)
    return weights, (weights * (grad_weights - row_inner)).astype(jnp.bfloat16)


def start_blocks(me, blocks, kv_all, sems):
    rows = blocks[0].shape[0]
    copies = []
    for k, block in enumerate(blocks):
        owner = lax.bitwise_xor(me, k)
        at = pl.ds(pl.multiple_of(owner * rows, rows), rows)
        copies.append(pltpu.make_async_copy(block, kv_all.at[at], sems.at[k]))
        copies[-1].start()
    return copies


def terms_kernel(n_ctx, heads, reach, docs, table_in, own_in, other_in, *refs):
    blocks, outs, scratch = refs[:n_ctx], refs[n_ctx : 2 * n_ctx], refs[2 * n_ctx :]
    table, qg_all, kv_all, key_win, value_win, terms, bf_buf, in_sem, out_sem, table_sem = scratch
    me, head = lax.axis_index("ctx"), lax.axis_index("head")
    both, width = blocks[0].shape
    tok_rows = both // 2
    runs_here = tok_rows // RUN
    run_rows = RUN * heads
    rows_here = tok_rows * heads

    table_copy = pltpu.make_async_copy(table_in, table, table_sem)
    table_copy.start()
    copies = start_blocks(me, blocks, kv_all, in_sem)
    for i, (source, part) in enumerate(((own_in, head), (other_in, 1 - head))):
        for w in range(2):
            for r in range(runs_here):
                at = pl.ds(pl.multiple_of(part * run_rows, run_rows), run_rows)
                copies.append(
                    pltpu.make_async_copy(
                        source.at[pl.ds(w * rows_here + r * run_rows, run_rows)],
                        qg_all.at[w, r, at],
                        in_sem.at[n_ctx + (i * 2 + w) * runs_here + r],
                    )
                )
                copies[-1].start()
    terms[...] = jnp.zeros_like(terms)
    table_copy.wait()
    for copy in copies:
        copy.wait()

    for r in range(runs_here):
        rows = run_window(table, kv_all, key_win, value_win, r, reach, runs_here, tok_rows)
        q_rows, g_rows = qg_all[0, r], qg_all[1, r]
        raw, one_over = weights_of(table, key_win[r], q_rows, r, reach, runs_here, docs, heads)
        weights, grad_scores = score_gradients(raw, one_over, value_win[r], g_rows)
        value_part = contract(weights.astype(jnp.bfloat16), g_rows, 1, 0)
        key_part = contract(grad_scores, q_rows, 1, 0) * (1.0 / math.sqrt(width))
        for j, row in enumerate(rows):
            part = slice(j * RUN, (j + 1) * RUN)
            terms[pl.ds(row, RUN), :] += key_part[part, :]
            terms[pl.ds(row + tok_rows, RUN), :] += value_part[part, :]

    out_copies = []
    for k in range(n_ctx):
        owner = lax.bitwise_xor(me, k)
        at = pl.ds(pl.multiple_of(owner * both, both), both)
        if outs[k].dtype == jnp.bfloat16:
            bf_buf[k] = terms[at, :].astype(jnp.bfloat16)
            source = bf_buf.at[k]
        else:
            source = terms.at[at]
        out_copies.append(pltpu.make_async_copy(source, outs[k], out_sem.at[k]))
        out_copies[-1].start()
    for copy in out_copies:
        copy.wait()


def gradient_terms(table, own, other, blocks, heads, reach, docs, seq_total):
    n_ctx = len(blocks)
    both, width = blocks[0].shape
    tok_rows = both // 2
    runs_here = tok_rows // RUN
    outs = []
    for k in range(n_ctx):
        leaves_first = goes_first_over_y(k) or k in (1, 2, 3)
        outs.append(jax.ShapeDtypeStruct((both, width), jnp.bfloat16 if leaves_first else jnp.float32))
    return pl.pallas_call(
        functools.partial(terms_kernel, n_ctx, heads, reach, docs),
        out_shape=outs,
        in_specs=[ANY] * (3 + n_ctx),
        out_specs=[ANY] * n_ctx,
        scratch_shapes=[
            pltpu.SMEM(table.shape, jnp.int32),
            pltpu.VMEM((2, runs_here, 2 * RUN * heads, width), jnp.bfloat16),
            pltpu.VMEM((n_ctx * both, width), jnp.bfloat16),
            pltpu.VMEM((runs_here, reach * RUN, width), jnp.bfloat16),
            pltpu.VMEM((runs_here, reach * RUN, width), jnp.bfloat16),
            pltpu.VMEM((n_ctx * both, width), jnp.float32),
            pltpu.VMEM((n_ctx, both, width), jnp.bfloat16),
            pltpu.SemaphoreType.DMA((n_ctx + 4 * runs_here,)),
            pltpu.SemaphoreType.DMA((n_ctx,)),
            pltpu.SemaphoreType.DMA,
        ],
        compiler_params=limit(seq_total),
    )(table, own, other, *blocks)


def rows_kernel(n_after, n_ctx, heads, reach, docs, table_in, own_in, *refs):
    refs = refs[n_after:]
    blocks, (att_out, qg_out), scratch = refs[:n_ctx], refs[n_ctx : n_ctx + 2], refs[n_ctx + 2 :]
    table, qg_all, kv_all, key_win, value_win, att_buf, grad_buf, in_sem, out_sem, table_sem = scratch
    me = lax.axis_index("ctx")
    both, width = blocks[0].shape
    tok_rows = both // 2
    runs_here = tok_rows // RUN
    run_rows = RUN * heads
    rows_here = tok_rows * heads

    table_copy = pltpu.make_async_copy(table_in, table, table_sem)
    table_copy.start()
    copies = start_blocks(me, blocks, kv_all, in_sem)
    copies.append(pltpu.make_async_copy(own_in, qg_all, in_sem.at[n_ctx]))
    copies[-1].start()
    table_copy.wait()
    for copy in copies:
        copy.wait()

    out_copies = []
    for r in range(runs_here):
        run_window(table, kv_all, key_win, value_win, r, reach, runs_here, tok_rows)
        here = slice(r * run_rows, (r + 1) * run_rows)
        q_rows = qg_all[here, :]
        g_rows = qg_all[rows_here + r * run_rows : rows_here + (r + 1) * run_rows, :]
        raw, one_over = weights_of(table, key_win[r], q_rows, r, reach, runs_here, docs, heads)
        attended = contract(value_win[r], raw.astype(jnp.bfloat16), 0, 0) * one_over
        att_buf[here, :] = attended.T.astype(jnp.bfloat16)
        _, grad_scores = score_gradients(raw, one_over, value_win[r], g_rows)
        query_part = contract(key_win[r], grad_scores, 0, 0) * (1.0 / math.sqrt(width))
        grad_buf[here, :] = query_part.T.astype(jnp.bfloat16)
        for i, (source, out) in enumerate(((att_buf, att_out), (grad_buf, qg_out))):
            at = pl.ds(r * run_rows, run_rows)
            out_copies.append(pltpu.make_async_copy(source.at[at], out.at[at], out_sem.at[2 * r + i]))
            out_copies[-1].start()
    for copy in out_copies:
        copy.wait()


def query_side(table, own, after, blocks, heads, reach, docs, seq_total):
    n_ctx = len(blocks)
    both, width = blocks[0].shape
    tok_rows = both // 2
    runs_here = tok_rows // RUN
    rows = own.shape[0] // 2
    return pl.pallas_call(
        functools.partial(rows_kernel, len(after), n_ctx, heads, reach, docs),
        out_shape=[jax.ShapeDtypeStruct((rows, width), jnp.bfloat16)] * 2,
        in_specs=[ANY] * (2 + len(after) + n_ctx),
        out_specs=[HBM] * 2,
        scratch_shapes=[
            pltpu.SMEM(table.shape, jnp.int32),
            pltpu.VMEM((2 * rows, width), jnp.bfloat16),
            pltpu.VMEM((n_ctx * both, width), jnp.bfloat16),
            pltpu.VMEM((runs_here, reach * RUN, width), jnp.bfloat16),
            pltpu.VMEM((runs_here, reach * RUN, width), jnp.bfloat16),
            pltpu.VMEM((rows, width), jnp.bfloat16),
            pltpu.VMEM((rows, width), jnp.bfloat16),
            pltpu.SemaphoreType.DMA((n_ctx + 1,)),
            pltpu.SemaphoreType.DMA((2 * runs_here,)),
            pltpu.SemaphoreType.DMA,
        ],
        compiler_params=limit(seq_total),
    )(table, own, *after, *blocks)


def body(n_ctx, n_head, queries, key_rows, value_rows, out_grad, doc_lengths, balance):
    tok_rows, heads, width = queries.shape
    seq_total = balance.shape[0]
    docs = doc_lengths.shape[0]
    runs_here = tok_rows // RUN
    reach = seq_total // LONGEST_SHARE // RUN + 1

    def swap(array, k):
        return lax.ppermute(array, "ctx", [(i, i ^ k) for i in range(n_ctx)])

    mine, own = pack(
        key_rows,
        value_rows,
        queries.reshape(tok_rows * heads, width),
        out_grad.reshape(tok_rows * heads, width),
        seq_total,
    )
    blocks = {0: mine}
    direct = [k for k in range(n_ctx - 1, 0, -1) if not goes_first_over_y(k)]
    for k in direct:
        blocks[k] = swap(mine, k)
    other = lax.ppermute(own, "head", [(i, n_head - 1 - i) for i in range(n_head)])
    for k in reversed(direct):
        if goes_first_over_y(k + 1):
            blocks[k + 1] = swap(blocks[k], 1)
    blocks = [blocks[k] for k in range(n_ctx)]

    place = jnp.stack([lax.axis_index("ctx"), lax.axis_index("head")]).astype(jnp.int32)
    table = make_table(place, balance, doc_lengths, blocks[1], runs_here, reach)
    terms = gradient_terms(table, own, other, blocks, heads, reach, docs, seq_total)

    far = [k for k in range(n_ctx - 2, 2, -2)]
    arrived = {k: swap(terms[k + 1], 1) for k in far}
    total = terms[0]
    for k in (2, 3, 1):
        total = total + swap(terms[k], k).astype(jnp.float32)
    after = []
    for k in far:
        pair = (terms[k] + arrived[k].astype(jnp.float32)).astype(jnp.bfloat16)
        total = total + swap(pair, k).astype(jnp.float32)
        after.append(pair)
    attended, query_grad = query_side(table, own, after, blocks, heads, reach, docs, seq_total)
    combined = total.astype(jnp.bfloat16)
    return (
        attended.reshape(tok_rows, heads, width),
        query_grad.reshape(tok_rows, heads, width),
        combined[:tok_rows],
        combined[tok_rows:],
    )


def solution(mesh):
    return jax.shard_map(
        functools.partial(body, mesh.shape["ctx"], mesh.shape["head"]),
        mesh=mesh,
        in_specs=(
            P(("seq", "ctx"), "head", None),
            P(("seq", "ctx"), None),
            P(("seq", "ctx"), None),
            P(("seq", "ctx"), "head", None),
            P("seq"),
            P("seq"),
        ),
        out_specs=(
            P(("seq", "ctx"), "head", None),
            P(("seq", "ctx"), "head", None),
            P(("seq", "ctx"), None),
            P(("seq", "ctx"), None),
        ),
        check_vma=False,
    )
```

```python
import functools
import math

import jax
import jax.numpy as jnp
from jax import lax
from jax.experimental import pallas as pl
from jax.experimental.pallas import tpu as pltpu
from jax.sharding import PartitionSpec as P

NEGATIVE = -1e30
RUN = 64
LONGEST_SHARE = 4

ANY = pl.BlockSpec(memory_space=pl.ANY)
VMEM = pl.BlockSpec(memory_space=pltpu.VMEM)
HBM = pl.BlockSpec(memory_space=pltpu.HBM)


def contract(a, b, dim_a, dim_b):
    return lax.dot_general(
        a, b, (((dim_a,), (dim_b,)), ((), ())), preferred_element_type=jnp.float32
    )


def limit(seq_total):
    return pltpu.CompilerParams(vmem_limit_bytes=(16 << 20) if seq_total <= 1024 else (56 << 20))


NEAR = (1, 2, 3, 4)


def high_bits(n_ctx):
    return [(1 << b, range(1 << b)) for b in range(3, n_ctx.bit_length() - 1)]


BLOCK_ORDER = (0, 4, 1, 2, 3, 7, 6, 5)
FAR_ORDER = (7, 6, 5)
SUM_ORDER = (4, 2, 3, 1)


def pack_kernel(key_rows, value_rows, q_rows, g_rows, balance, doc_lengths, kv_out, qg_out, balance_out, docs_out, sems):
    tok_rows, rows = key_rows.shape[0], q_rows.shape[0]
    copies = [
        pltpu.make_async_copy(key_rows, kv_out.at[pl.ds(0, tok_rows)], sems.at[0]),
        pltpu.make_async_copy(value_rows, kv_out.at[pl.ds(tok_rows, tok_rows)], sems.at[1]),
        pltpu.make_async_copy(q_rows, qg_out.at[pl.ds(0, rows)], sems.at[2]),
        pltpu.make_async_copy(g_rows, qg_out.at[pl.ds(rows, rows)], sems.at[3]),
        pltpu.make_async_copy(balance, balance_out, sems.at[4]),
        pltpu.make_async_copy(doc_lengths, docs_out, sems.at[5]),
    ]
    for copy in copies:
        copy.start()
    for copy in copies:
        copy.wait()


def pack(key_rows, value_rows, q_rows, g_rows, balance, doc_lengths):
    return pl.pallas_call(
        pack_kernel,
        out_shape=[
            jax.ShapeDtypeStruct((2 * key_rows.shape[0], key_rows.shape[1]), jnp.bfloat16),
            jax.ShapeDtypeStruct((2 * q_rows.shape[0], q_rows.shape[1]), jnp.bfloat16),
            jax.ShapeDtypeStruct(balance.shape, jnp.int32),
            jax.ShapeDtypeStruct(doc_lengths.shape, jnp.int32),
        ],
        in_specs=[ANY] * 6,
        out_specs=[ANY] * 4,
        scratch_shapes=[pltpu.SemaphoreType.DMA((6,))],
        compiler_params=limit(balance.shape[0]),
    )(
        *[
            pltpu.with_memory_space_constraint(a, pltpu.HBM)
            for a in (key_rows, value_rows, q_rows, g_rows, balance, doc_lengths)
        ]
    )


def start_lists(balance_in, docs_in, lists):
    balance, doc_lengths, _, sems = lists
    copies = [
        pltpu.make_async_copy(balance_in, balance, sems.at[0]),
        pltpu.make_async_copy(docs_in, doc_lengths, sems.at[1]),
    ]
    for copy in copies:
        copy.start()
    return copies


def finish_lists(copies, lists):
    balance, _, slot_of, _ = lists
    runs = slot_of.shape[0]
    for copy in copies:
        copy.wait()

    def note(s, carry):
        slot_of[lax.shift_right_logical(balance[s * RUN], 6)] = s
        return carry

    lax.fori_loop(0, runs, note, 0, unroll=runs <= 16)


def run_window(me, lists, kv_all, key_win, value_win, r, reach, runs_here, tok_rows):
    balance, _, slot_of, _ = lists
    place_run = lax.shift_right_logical(balance[(me * runs_here + r) * RUN], 6)
    rows = []
    for j in range(reach):
        slot = slot_of[jnp.maximum(place_run - (reach - 1) + j, 0)]
        row = lax.div(slot, runs_here) * (2 * tok_rows) + lax.rem(slot, runs_here) * RUN
        row = pl.multiple_of(row, RUN)
        rows.append(row)
        key_win[r, j * RUN : (j + 1) * RUN, :] = kv_all[pl.ds(row, RUN), :]
        value_win[r, j * RUN : (j + 1) * RUN, :] = kv_all[pl.ds(row + tok_rows, RUN), :]
    return place_run, rows


def weights_of(doc_lengths, place_run, keys, q_rows, reach, heads):
    count = q_rows.shape[0]
    scaling = math.log2(math.e) / math.sqrt(keys.shape[1])
    lane = lax.broadcasted_iota(jnp.int32, (1, count), 1)
    q_off = lax.div(lax.rem(lane, RUN * heads), heads)
    q_pos = place_run * RUN + q_off
    doc_start = jnp.zeros_like(q_pos)
    doc_end = jnp.int32(0)
    for d in range(doc_lengths.shape[0]):
        doc_end = doc_end + doc_lengths[d]
        doc_start = jnp.where(doc_end <= q_pos, doc_end, doc_start)
    doc_start = doc_start - (place_run - (reach - 1)) * RUN
    scores = contract(keys, q_rows, 1, 1)
    early = (reach - 1) * RUN
    k_early = lax.broadcasted_iota(jnp.int32, (early, count), 0)
    k_own = lax.broadcasted_iota(jnp.int32, (RUN, count), 0)
    scores = jnp.concatenate(
        [
            jnp.where(k_early >= doc_start, scores[:early], NEGATIVE),
            jnp.where((k_own + early >= doc_start) & (k_own <= q_off), scores[early:], NEGATIVE),
        ],
        axis=0,
    )
    top = jnp.max(scores, axis=0, keepdims=True)
    raw = jnp.exp2((scores - top) * scaling)
    return raw, 1.0 / jnp.sum(raw, axis=0, keepdims=True)


def score_gradients(raw, one_over, values, g_rows):
    weights = raw * one_over
    grad_weights = contract(values, g_rows, 1, 1)
    row_inner = jnp.sum(weights * grad_weights, axis=0, keepdims=True)
    return weights, (weights * (grad_weights - row_inner)).astype(jnp.bfloat16)


def load_blocks(me, listed, blocks, kv_all):
    rows = blocks[0].shape[0]
    for k, block in zip(listed, blocks):
        owner = lax.bitwise_xor(me, k)
        kv_all[pl.ds(pl.multiple_of(owner * rows, rows), rows), :] = block[...]


def terms_kernel(listed, heads, reach, balance_in, docs_in, own_in, other_in, *refs):
    n_ctx = len(listed)
    blocks, outs, scratch = refs[:n_ctx], refs[n_ctx : 2 * n_ctx], refs[2 * n_ctx :]
    qg_all, kv_all, key_win, value_win, terms, *lists = scratch
    me, head = lax.axis_index("ctx"), lax.axis_index("head")
    both, width = blocks[0].shape
    tok_rows = both // 2
    runs_here = tok_rows // RUN
    run_rows = RUN * heads
    rows_here = tok_rows * heads

    copies = start_lists(balance_in, docs_in, lists)
    load_blocks(me, listed, blocks, kv_all)
    for source, part in ((own_in, head), (other_in, 1 - head)):
        at = pl.ds(pl.multiple_of(part * run_rows, run_rows), run_rows)
        for w in range(2):
            for r in range(runs_here):
                here = w * rows_here + r * run_rows
                qg_all[w, r, at, :] = source[here : here + run_rows, :]
    terms[...] = jnp.zeros_like(terms)
    finish_lists(copies, lists)

    for r in range(runs_here):
        place_run, rows = run_window(me, lists, kv_all, key_win, value_win, r, reach, runs_here, tok_rows)
        q_rows, g_rows = qg_all[0, r], qg_all[1, r]
        raw, one_over = weights_of(lists[1], place_run, key_win[r], q_rows, reach, heads)
        weights, grad_scores = score_gradients(raw, one_over, value_win[r], g_rows)
        value_part = contract(weights.astype(jnp.bfloat16), g_rows, 1, 0)
        key_part = contract(grad_scores, q_rows, 1, 0) * (1.0 / math.sqrt(width))
        for j, row in enumerate(rows):
            part = slice(j * RUN, (j + 1) * RUN)
            terms[pl.ds(row, RUN), :] += key_part[part, :]
            terms[pl.ds(row + tok_rows, RUN), :] += value_part[part, :]

    for k in range(n_ctx):
        owner = lax.bitwise_xor(me, k)
        at = pl.ds(pl.multiple_of(owner * both, both), both)
        outs[k][...] = terms[at, :].astype(outs[k].dtype)


def gradient_terms(balance, doc_lengths, own, other, blocks, heads, reach):
    listed, blocks = zip(*blocks)
    n_ctx = len(blocks)
    both, width = blocks[0].shape
    tok_rows = both // 2
    runs_here = tok_rows // RUN
    kept = [k for k in range(n_ctx) if k in (0, 4) or 8 <= k < n_ctx // 2 or k < min(8, n_ctx // 2) and n_ctx > 8]
    outs = [
        jax.ShapeDtypeStruct((both, width), jnp.float32 if k in kept else jnp.bfloat16) for k in range(n_ctx)
    ]
    return pl.pallas_call(
        functools.partial(terms_kernel, listed, heads, reach),
        out_shape=outs,
        in_specs=[ANY] * 2 + [VMEM] * (2 + n_ctx),
        out_specs=[VMEM] * n_ctx,
        scratch_shapes=[
            pltpu.VMEM((2, runs_here, 2 * RUN * heads, width), jnp.bfloat16),
            pltpu.VMEM((n_ctx * both, width), jnp.bfloat16),
            pltpu.VMEM((runs_here, reach * RUN, width), jnp.bfloat16),
            pltpu.VMEM((runs_here, reach * RUN, width), jnp.bfloat16),
            pltpu.VMEM((n_ctx * both, width), jnp.float32),
            pltpu.SMEM(balance.shape, jnp.int32),
            pltpu.SMEM(doc_lengths.shape, jnp.int32),
            pltpu.SMEM((balance.shape[0] // RUN,), jnp.int32),
            pltpu.SemaphoreType.DMA((2,)),
        ],
        compiler_params=limit(balance.shape[0]),
    )(balance, doc_lengths, own, other, *blocks)


def rows_kernel(n_after, listed, heads, reach, balance_in, docs_in, own_in, *refs):
    refs = refs[n_after:]
    n_ctx = len(listed)
    blocks, (att_out, qg_out), scratch = refs[:n_ctx], refs[n_ctx : n_ctx + 2], refs[n_ctx + 2 :]
    kv_all, key_win, value_win, att_buf, grad_buf, out_sem, *lists = scratch
    me = lax.axis_index("ctx")
    both, width = blocks[0].shape
    tok_rows = both // 2
    runs_here = tok_rows // RUN
    run_rows = RUN * heads
    rows_here = tok_rows * heads

    copies = start_lists(balance_in, docs_in, lists)
    load_blocks(me, listed, blocks, kv_all)
    finish_lists(copies, lists)

    out_copies = []
    for r in range(runs_here):
        place_run, _ = run_window(me, lists, kv_all, key_win, value_win, r, reach, runs_here, tok_rows)
        here = slice(r * run_rows, (r + 1) * run_rows)
        q_rows = own_in[here, :]
        g_rows = own_in[rows_here + r * run_rows : rows_here + (r + 1) * run_rows, :]
        raw, one_over = weights_of(lists[1], place_run, key_win[r], q_rows, reach, heads)
        attended = contract(value_win[r], raw.astype(jnp.bfloat16), 0, 0) * one_over
        att_buf[here, :] = attended.T.astype(jnp.bfloat16)
        _, grad_scores = score_gradients(raw, one_over, value_win[r], g_rows)
        query_part = contract(key_win[r], grad_scores, 0, 0) * (1.0 / math.sqrt(width))
        grad_buf[here, :] = query_part.T.astype(jnp.bfloat16)
        for i, (source, out) in enumerate(((att_buf, att_out), (grad_buf, qg_out))):
            at = pl.ds(r * run_rows, run_rows)
            out_copies.append(pltpu.make_async_copy(source.at[at], out.at[at], out_sem.at[2 * r + i]))
            out_copies[-1].start()
    for copy in out_copies:
        copy.wait()


def query_side(balance, doc_lengths, own, after, blocks, heads, reach):
    listed, blocks = zip(*blocks)
    n_ctx = len(blocks)
    both, width = blocks[0].shape
    tok_rows = both // 2
    runs_here = tok_rows // RUN
    rows = own.shape[0] // 2
    return pl.pallas_call(
        functools.partial(rows_kernel, len(after), listed, heads, reach),
        out_shape=[jax.ShapeDtypeStruct((rows, width), jnp.bfloat16)] * 2,
        in_specs=[ANY, ANY, VMEM] + [ANY] * len(after) + [VMEM] * n_ctx,
        out_specs=[HBM] * 2,
        scratch_shapes=[
            pltpu.VMEM((n_ctx * both, width), jnp.bfloat16),
            pltpu.VMEM((runs_here, reach * RUN, width), jnp.bfloat16),
            pltpu.VMEM((runs_here, reach * RUN, width), jnp.bfloat16),
            pltpu.VMEM((rows, width), jnp.bfloat16),
            pltpu.VMEM((rows, width), jnp.bfloat16),
            pltpu.SemaphoreType.DMA((2 * runs_here,)),
            pltpu.SMEM(balance.shape, jnp.int32),
            pltpu.SMEM(doc_lengths.shape, jnp.int32),
            pltpu.SMEM((balance.shape[0] // RUN,), jnp.int32),
            pltpu.SemaphoreType.DMA((2,)),
        ],
        compiler_params=limit(balance.shape[0]),
    )(balance, doc_lengths, own, *after, *blocks)


def body(n_ctx, n_head, queries, key_rows, value_rows, out_grad, doc_lengths, balance):
    tok_rows, heads, width = queries.shape
    seq_total = balance.shape[0]
    reach = seq_total // LONGEST_SHARE // RUN + 1

    def swap(array, k):
        return lax.ppermute(array, "ctx", [(i, i ^ k) for i in range(n_ctx)])

    mine, own, balance, doc_lengths = pack(
        key_rows,
        value_rows,
        queries.reshape(tok_rows * heads, width),
        out_grad.reshape(tok_rows * heads, width),
        balance,
        doc_lengths,
    )
    blocks = {0: mine}
    other = lax.ppermute(own, "head", [(i, n_head - 1 - i) for i in range(n_head)])
    for k in (4, 1, 2, 3):
        blocks[k] = swap(mine, k)
    for k in FAR_ORDER:
        blocks[k] = swap(blocks[4], k - 4)
    for bit, below in high_bits(n_ctx):
        for k in below:
            blocks[bit + k] = swap(blocks[k], bit)

    listed = BLOCK_ORDER + tuple(range(8, n_ctx))
    blocks = [(k, blocks[k]) for k in listed]
    terms = list(gradient_terms(balance, doc_lengths, own, other, blocks, heads, reach))

    for bit, below in reversed(high_bits(n_ctx)):
        for k in below:
            terms[k] = terms[k] + swap(terms[bit + k].astype(jnp.bfloat16), bit).astype(jnp.float32)
    far = terms[4]
    for k in FAR_ORDER:
        far = far + swap(terms[k].astype(jnp.bfloat16), k - 4).astype(jnp.float32)
    far = far.astype(jnp.bfloat16)
    total = terms[0]
    for k in SUM_ORDER:
        term = far if k == 4 else terms[k].astype(jnp.bfloat16)
        total = total + swap(term, k).astype(jnp.float32)
    after = [far]
    attended, query_grad = query_side(balance, doc_lengths, own, after, blocks, heads, reach)
    combined = total.astype(jnp.bfloat16)
    return (
        attended.reshape(tok_rows, heads, width),
        query_grad.reshape(tok_rows, heads, width),
        combined[:tok_rows],
        combined[tok_rows:],
    )


def solution(mesh):
    return jax.shard_map(
        functools.partial(body, mesh.shape["ctx"], mesh.shape["head"]),
        mesh=mesh,
        in_specs=(
            P(("seq", "ctx"), "head", None),
            P(("seq", "ctx"), None),
            P(("seq", "ctx"), None),
            P(("seq", "ctx"), "head", None),
            P("seq"),
            P("seq"),
        ),
        out_specs=(
            P(("seq", "ctx"), "head", None),
            P(("seq", "ctx"), "head", None),
            P(("seq", "ctx"), None),
            P(("seq", "ctx"), None),
        ),
        check_vma=False,
    )
```

```python
import functools
import math

import jax
import jax.numpy as jnp
from jax import lax
from jax.experimental import pallas as pl
from jax.experimental.pallas import tpu as pltpu
from jax.sharding import PartitionSpec as P

NEGATIVE = -1e30
RUN = 64
LONGEST_SHARE = 4

ANY = pl.BlockSpec(memory_space=pl.ANY)
VMEM = pl.BlockSpec(memory_space=pltpu.VMEM)
HBM = pl.BlockSpec(memory_space=pltpu.HBM)


def contract(a, b, dim_a, dim_b):
    return lax.dot_general(
        a, b, (((dim_a,), (dim_b,)), ((), ())), preferred_element_type=jnp.float32
    )


def limit(seq_total):
    return pltpu.CompilerParams(vmem_limit_bytes=(16 << 20) if seq_total <= 1024 else (56 << 20))


GATHER_FROM = {1: 0, 2: 0, 3: 0, 4: 0, 5: 4, 6: 4, 7: 4}
SCATTER_OVER = {1: 0, 2: 0, 3: 0, 4: 0, 5: 4, 6: 4, 7: 4}
BLOCK_ORDER = (0, 6, 3, 5, 2, 4, 1, 7)
GATHER_ORDER = (4, 1, 2, 3, 6, 5, 7)
SUM_ORDER = (4, 3, 1, 2, 7, 6, 5)


def high_bits(n_ctx):
    return [(1 << b, range(1 << b)) for b in range(3, n_ctx.bit_length() - 1)]


def pack_kernel(key_rows, value_rows, q_rows, g_rows, balance, doc_lengths, kv_out, qg_out, balance_out, docs_out, sems):
    tok_rows, rows = key_rows.shape[0], q_rows.shape[0]
    copies = [
        pltpu.make_async_copy(key_rows, kv_out.at[pl.ds(0, tok_rows)], sems.at[0]),
        pltpu.make_async_copy(value_rows, kv_out.at[pl.ds(tok_rows, tok_rows)], sems.at[1]),
        pltpu.make_async_copy(q_rows, qg_out.at[pl.ds(0, rows)], sems.at[2]),
        pltpu.make_async_copy(g_rows, qg_out.at[pl.ds(rows, rows)], sems.at[3]),
        pltpu.make_async_copy(balance, balance_out, sems.at[4]),
        pltpu.make_async_copy(doc_lengths, docs_out, sems.at[5]),
    ]
    for copy in copies:
        copy.start()
    for copy in copies:
        copy.wait()


def pack(key_rows, value_rows, q_rows, g_rows, balance, doc_lengths):
    return pl.pallas_call(
        pack_kernel,
        out_shape=[
            jax.ShapeDtypeStruct((2 * key_rows.shape[0], key_rows.shape[1]), jnp.bfloat16),
            jax.ShapeDtypeStruct((2 * q_rows.shape[0], q_rows.shape[1]), jnp.bfloat16),
            jax.ShapeDtypeStruct(balance.shape, jnp.int32),
            jax.ShapeDtypeStruct(doc_lengths.shape, jnp.int32),
        ],
        in_specs=[ANY] * 6,
        out_specs=[ANY] * 4,
        scratch_shapes=[pltpu.SemaphoreType.DMA((6,))],
        compiler_params=limit(balance.shape[0]),
    )(
        *[
            pltpu.with_memory_space_constraint(a, pltpu.HBM)
            for a in (key_rows, value_rows, q_rows, g_rows, balance, doc_lengths)
        ]
    )


def start_lists(balance_in, docs_in, lists):
    balance, doc_lengths, _, sems = lists
    copies = [
        pltpu.make_async_copy(balance_in, balance, sems.at[0]),
        pltpu.make_async_copy(docs_in, doc_lengths, sems.at[1]),
    ]
    for copy in copies:
        copy.start()
    return copies


def finish_lists(copies, lists):
    balance, _, slot_of, _ = lists
    runs = slot_of.shape[0]
    for copy in copies:
        copy.wait()

    def note(s, carry):
        slot_of[lax.shift_right_logical(balance[s * RUN], 6)] = s
        return carry

    lax.fori_loop(0, runs, note, 0, unroll=runs <= 16)


def run_window(me, lists, kv_all, key_win, value_win, r, reach, runs_here, tok_rows):
    balance, _, slot_of, _ = lists
    place_run = lax.shift_right_logical(balance[(me * runs_here + r) * RUN], 6)
    rows = []
    for j in range(reach):
        slot = slot_of[jnp.maximum(place_run - (reach - 1) + j, 0)]
        row = lax.div(slot, runs_here) * (2 * tok_rows) + lax.rem(slot, runs_here) * RUN
        row = pl.multiple_of(row, RUN)
        rows.append(row)
        key_win[r, j * RUN : (j + 1) * RUN, :] = kv_all[pl.ds(row, RUN), :]
        value_win[r, j * RUN : (j + 1) * RUN, :] = kv_all[pl.ds(row + tok_rows, RUN), :]
    return place_run, rows


def weights_of(doc_lengths, place_run, keys, q_rows, reach, heads):
    count = q_rows.shape[0]
    scaling = math.log2(math.e) / math.sqrt(keys.shape[1])
    lane = lax.broadcasted_iota(jnp.int32, (1, count), 1)
    q_off = lax.div(lax.rem(lane, RUN * heads), heads)
    q_pos = place_run * RUN + q_off
    doc_start = jnp.zeros_like(q_pos)
    doc_end = jnp.int32(0)
    for d in range(doc_lengths.shape[0]):
        doc_end = doc_end + doc_lengths[d]
        doc_start = jnp.where(doc_end <= q_pos, doc_end, doc_start)
    doc_start = doc_start - (place_run - (reach - 1)) * RUN
    scores = contract(keys, q_rows, 1, 1)
    early = (reach - 1) * RUN
    k_early = lax.broadcasted_iota(jnp.int32, (early, count), 0)
    k_own = lax.broadcasted_iota(jnp.int32, (RUN, count), 0)
    scores = jnp.concatenate(
        [
            jnp.where(k_early >= doc_start, scores[:early], NEGATIVE),
            jnp.where((k_own + early >= doc_start) & (k_own <= q_off), scores[early:], NEGATIVE),
        ],
        axis=0,
    )
    top = jnp.max(scores, axis=0, keepdims=True)
    raw = jnp.exp2((scores - top) * scaling)
    return raw, 1.0 / jnp.sum(raw, axis=0, keepdims=True)


def score_gradients(raw, one_over, values, g_rows):
    weights = raw * one_over
    grad_weights = contract(values, g_rows, 1, 1)
    row_inner = jnp.sum(weights * grad_weights, axis=0, keepdims=True)
    return weights, (weights * (grad_weights - row_inner)).astype(jnp.bfloat16)


def load_blocks(me, listed, blocks, kv_all):
    rows = blocks[0].shape[0]
    for k, block in zip(listed, blocks):
        owner = lax.bitwise_xor(me, k)
        kv_all[pl.ds(pl.multiple_of(owner * rows, rows), rows), :] = block[...]


def terms_kernel(listed, heads, reach, balance_in, docs_in, own_in, other_in, *refs):
    n_ctx = len(listed)
    blocks, outs, scratch = refs[:n_ctx], refs[n_ctx : 2 * n_ctx], refs[2 * n_ctx :]
    qg_all, kv_all, key_win, value_win, terms, *lists = scratch
    me, head = lax.axis_index("ctx"), lax.axis_index("head")
    both, width = blocks[0].shape
    tok_rows = both // 2
    runs_here = tok_rows // RUN
    run_rows = RUN * heads
    rows_here = tok_rows * heads

    copies = start_lists(balance_in, docs_in, lists)
    load_blocks(me, listed, blocks, kv_all)
    for source, part in ((own_in, head), (other_in, 1 - head)):
        at = pl.ds(pl.multiple_of(part * run_rows, run_rows), run_rows)
        for w in range(2):
            for r in range(runs_here):
                here = w * rows_here + r * run_rows
                qg_all[w, r, at, :] = source[here : here + run_rows, :]
    terms[...] = jnp.zeros_like(terms)
    finish_lists(copies, lists)

    for r in range(runs_here):
        place_run, rows = run_window(me, lists, kv_all, key_win, value_win, r, reach, runs_here, tok_rows)
        q_rows, g_rows = qg_all[0, r], qg_all[1, r]
        raw, one_over = weights_of(lists[1], place_run, key_win[r], q_rows, reach, heads)
        weights, grad_scores = score_gradients(raw, one_over, value_win[r], g_rows)
        value_part = contract(weights.astype(jnp.bfloat16), g_rows, 1, 0)
        key_part = contract(grad_scores, q_rows, 1, 0) * (1.0 / math.sqrt(width))
        for j, row in enumerate(rows):
            part = slice(j * RUN, (j + 1) * RUN)
            terms[pl.ds(row, RUN), :] += key_part[part, :]
            terms[pl.ds(row + tok_rows, RUN), :] += value_part[part, :]

    for k in range(n_ctx):
        owner = lax.bitwise_xor(me, k)
        at = pl.ds(pl.multiple_of(owner * both, both), both)
        outs[k][...] = terms[at, :].astype(outs[k].dtype)


def gradient_terms(balance, doc_lengths, own, other, blocks, heads, reach):
    listed, blocks = zip(*blocks)
    n_ctx = len(blocks)
    both, width = blocks[0].shape
    tok_rows = both // 2
    runs_here = tok_rows // RUN
    kept = [0, *SCATTER_OVER.values()] if n_ctx == 8 else range(n_ctx // 2)
    outs = [
        jax.ShapeDtypeStruct((both, width), jnp.float32 if k in kept else jnp.bfloat16) for k in range(n_ctx)
    ]
    return pl.pallas_call(
        functools.partial(terms_kernel, listed, heads, reach),
        out_shape=outs,
        in_specs=[ANY] * 2 + [VMEM] * (2 + n_ctx),
        out_specs=[VMEM] * n_ctx,
        scratch_shapes=[
            pltpu.VMEM((2, runs_here, 2 * RUN * heads, width), jnp.bfloat16),
            pltpu.VMEM((n_ctx * both, width), jnp.bfloat16),
            pltpu.VMEM((runs_here, reach * RUN, width), jnp.bfloat16),
            pltpu.VMEM((runs_here, reach * RUN, width), jnp.bfloat16),
            pltpu.VMEM((n_ctx * both, width), jnp.float32),
            pltpu.SMEM(balance.shape, jnp.int32),
            pltpu.SMEM(doc_lengths.shape, jnp.int32),
            pltpu.SMEM((balance.shape[0] // RUN,), jnp.int32),
            pltpu.SemaphoreType.DMA((2,)),
        ],
        compiler_params=limit(balance.shape[0]),
    )(balance, doc_lengths, own, other, *blocks)


def rows_kernel(n_after, listed, heads, reach, balance_in, docs_in, own_in, *refs):
    refs = refs[n_after:]
    n_ctx = len(listed)
    blocks, (att_out, qg_out), scratch = refs[:n_ctx], refs[n_ctx : n_ctx + 2], refs[n_ctx + 2 :]
    kv_all, key_win, value_win, att_buf, grad_buf, out_sem, *lists = scratch
    me = lax.axis_index("ctx")
    both, width = blocks[0].shape
    tok_rows = both // 2
    runs_here = tok_rows // RUN
    run_rows = RUN * heads
    rows_here = tok_rows * heads

    copies = start_lists(balance_in, docs_in, lists)
    load_blocks(me, listed, blocks, kv_all)
    finish_lists(copies, lists)

    out_copies = []
    for r in range(runs_here):
        place_run, _ = run_window(me, lists, kv_all, key_win, value_win, r, reach, runs_here, tok_rows)
        here = slice(r * run_rows, (r + 1) * run_rows)
        q_rows = own_in[here, :]
        g_rows = own_in[rows_here + r * run_rows : rows_here + (r + 1) * run_rows, :]
        raw, one_over = weights_of(lists[1], place_run, key_win[r], q_rows, reach, heads)
        attended = contract(value_win[r], raw.astype(jnp.bfloat16), 0, 0) * one_over
        att_buf[here, :] = attended.T.astype(jnp.bfloat16)
        _, grad_scores = score_gradients(raw, one_over, value_win[r], g_rows)
        query_part = contract(key_win[r], grad_scores, 0, 0) * (1.0 / math.sqrt(width))
        grad_buf[here, :] = query_part.T.astype(jnp.bfloat16)
        for i, (source, out) in enumerate(((att_buf, att_out), (grad_buf, qg_out))):
            at = pl.ds(r * run_rows, run_rows)
            out_copies.append(pltpu.make_async_copy(source.at[at], out.at[at], out_sem.at[2 * r + i]))
            out_copies[-1].start()
    for copy in out_copies:
        copy.wait()


def query_side(balance, doc_lengths, own, after, blocks, heads, reach):
    listed, blocks = zip(*blocks)
    n_ctx = len(blocks)
    both, width = blocks[0].shape
    tok_rows = both // 2
    runs_here = tok_rows // RUN
    rows = own.shape[0] // 2
    return pl.pallas_call(
        functools.partial(rows_kernel, len(after), listed, heads, reach),
        out_shape=[jax.ShapeDtypeStruct((rows, width), jnp.bfloat16)] * 2,
        in_specs=[ANY, ANY, VMEM] + [ANY] * len(after) + [VMEM] * n_ctx,
        out_specs=[HBM] * 2,
        scratch_shapes=[
            pltpu.VMEM((n_ctx * both, width), jnp.bfloat16),
            pltpu.VMEM((runs_here, reach * RUN, width), jnp.bfloat16),
            pltpu.VMEM((runs_here, reach * RUN, width), jnp.bfloat16),
            pltpu.VMEM((rows, width), jnp.bfloat16),
            pltpu.VMEM((rows, width), jnp.bfloat16),
            pltpu.SemaphoreType.DMA((2 * runs_here,)),
            pltpu.SMEM(balance.shape, jnp.int32),
            pltpu.SMEM(doc_lengths.shape, jnp.int32),
            pltpu.SMEM((balance.shape[0] // RUN,), jnp.int32),
            pltpu.SemaphoreType.DMA((2,)),
        ],
        compiler_params=limit(balance.shape[0]),
    )(balance, doc_lengths, own, *after, *blocks)


def body(n_ctx, n_head, queries, key_rows, value_rows, out_grad, doc_lengths, balance):
    tok_rows, heads, width = queries.shape
    seq_total = balance.shape[0]
    reach = seq_total // LONGEST_SHARE // RUN + 1

    def swap(array, k):
        return lax.ppermute(array, "ctx", [(i, i ^ k) for i in range(n_ctx)])

    mine, own, balance, doc_lengths = pack(
        key_rows,
        value_rows,
        queries.reshape(tok_rows * heads, width),
        out_grad.reshape(tok_rows * heads, width),
        balance,
        doc_lengths,
    )
    blocks = {0: mine}
    other = lax.ppermute(own, "head", [(i, n_head - 1 - i) for i in range(n_head)])
    for k in GATHER_ORDER:
        blocks[k] = swap(blocks[GATHER_FROM[k]], k ^ GATHER_FROM[k])
    for bit, below in high_bits(n_ctx):
        for k in below:
            blocks[bit + k] = swap(blocks[k], bit)

    listed = BLOCK_ORDER + tuple(range(8, n_ctx))
    blocks = [(k, blocks[k]) for k in listed]
    terms = list(gradient_terms(balance, doc_lengths, own, other, blocks, heads, reach))

    for bit, below in reversed(high_bits(n_ctx)):
        for k in below:
            terms[k] = terms[k] + swap(terms[bit + k].astype(jnp.bfloat16), bit).astype(jnp.float32)
    sums = {}

    def summed(k):
        total = terms[k]
        for child in SUM_ORDER:
            if SCATTER_OVER[child] == k:
                sums[child] = summed(child).astype(jnp.bfloat16)
                total = total + swap(sums[child], child ^ k).astype(jnp.float32)
        return total

    total = summed(0)
    after = [sums[k] for k in sums if k in SCATTER_OVER.values()]
    attended, query_grad = query_side(balance, doc_lengths, own, after, blocks, heads, reach)
    combined = total.astype(jnp.bfloat16)
    return (
        attended.reshape(tok_rows, heads, width),
        query_grad.reshape(tok_rows, heads, width),
        combined[:tok_rows],
        combined[tok_rows:],
    )


def solution(mesh):
    return jax.shard_map(
        functools.partial(body, mesh.shape["ctx"], mesh.shape["head"]),
        mesh=mesh,
        in_specs=(
            P(("seq", "ctx"), "head", None),
            P(("seq", "ctx"), None),
            P(("seq", "ctx"), None),
            P(("seq", "ctx"), "head", None),
            P("seq"),
            P("seq"),
        ),
        out_specs=(
            P(("seq", "ctx"), "head", None),
            P(("seq", "ctx"), "head", None),
            P(("seq", "ctx"), None),
            P(("seq", "ctx"), None),
        ),
        check_vma=False,
    )
```

```python
import functools
import math

import jax
import jax.numpy as jnp
from jax import lax
from jax.experimental import pallas as pl
from jax.experimental.pallas import tpu as pltpu
from jax.sharding import PartitionSpec as P

NEGATIVE = -1e30
RUN = 64
LONGEST_SHARE = 4

ANY = pl.BlockSpec(memory_space=pl.ANY)
VMEM = pl.BlockSpec(memory_space=pltpu.VMEM)
HBM = pl.BlockSpec(memory_space=pltpu.HBM)


def contract(a, b, dim_a, dim_b):
    return lax.dot_general(
        a, b, (((dim_a,), (dim_b,)), ((), ())), preferred_element_type=jnp.float32
    )


def limit(seq_total):
    return pltpu.CompilerParams(vmem_limit_bytes=(16 << 20) if seq_total <= 1024 else (56 << 20))


MERGED = (3,)
BLOCK_ORDER = (0, 6, 5, 2, 1, 4, 7, 3)
FAR_ORDER = (5, 6, 7)
BACK_ORDER = (7, 6, 5)
SUM_ORDER = (4, 3, 1, 2)


def high_bits(n_ctx):
    return [(1 << b, range(1 << b)) for b in range(3, n_ctx.bit_length() - 1)]


def join_kernel(first, second, out):
    rows = first.shape[0]
    out[:rows, :] = first[...]
    out[rows:, :] = second[...]


def join(first, second, seq_total):
    return pl.pallas_call(
        join_kernel,
        out_shape=jax.ShapeDtypeStruct((2 * first.shape[0], first.shape[1]), first.dtype),
        in_specs=[VMEM] * 2,
        out_specs=VMEM,
        compiler_params=limit(seq_total),
    )(first, second)


def pack_kernel(key_rows, value_rows, balance, doc_lengths, kv_out, balance_out, docs_out, sems):
    tok_rows = key_rows.shape[0]
    copies = [
        pltpu.make_async_copy(key_rows, kv_out.at[pl.ds(0, tok_rows)], sems.at[0]),
        pltpu.make_async_copy(value_rows, kv_out.at[pl.ds(tok_rows, tok_rows)], sems.at[1]),
        pltpu.make_async_copy(balance, balance_out, sems.at[2]),
        pltpu.make_async_copy(doc_lengths, docs_out, sems.at[3]),
    ]
    for copy in copies:
        copy.start()
    for copy in copies:
        copy.wait()


def pack(key_rows, value_rows, balance, doc_lengths):
    return pl.pallas_call(
        pack_kernel,
        out_shape=[
            jax.ShapeDtypeStruct((2 * key_rows.shape[0], key_rows.shape[1]), jnp.bfloat16),
            jax.ShapeDtypeStruct(balance.shape, jnp.int32),
            jax.ShapeDtypeStruct(doc_lengths.shape, jnp.int32),
        ],
        in_specs=[ANY] * 4,
        out_specs=[ANY] * 3,
        scratch_shapes=[pltpu.SemaphoreType.DMA((4,))],
        compiler_params=limit(balance.shape[0]),
    )(*[pltpu.with_memory_space_constraint(a, pltpu.HBM) for a in (key_rows, value_rows, balance, doc_lengths)])


def start_lists(balance_in, docs_in, lists):
    balance, doc_lengths, _, sems = lists
    copies = [
        pltpu.make_async_copy(balance_in, balance, sems.at[0]),
        pltpu.make_async_copy(docs_in, doc_lengths, sems.at[1]),
    ]
    for copy in copies:
        copy.start()
    return copies


def finish_lists(copies, lists):
    balance, _, slot_of, _ = lists
    runs = slot_of.shape[0]
    for copy in copies:
        copy.wait()

    def note(s, carry):
        slot_of[lax.shift_right_logical(balance[s * RUN], 6)] = s
        return carry

    lax.fori_loop(0, runs, note, 0, unroll=runs <= 16)


def run_window(me, lists, kv_all, key_win, value_win, r, reach, runs_here, tok_rows):
    balance, _, slot_of, _ = lists
    place_run = lax.shift_right_logical(balance[(me * runs_here + r) * RUN], 6)
    rows = []
    for j in range(reach):
        slot = slot_of[jnp.maximum(place_run - (reach - 1) + j, 0)]
        row = lax.div(slot, runs_here) * (2 * tok_rows) + lax.rem(slot, runs_here) * RUN
        row = pl.multiple_of(row, RUN)
        rows.append(row)
        key_win[r, j * RUN : (j + 1) * RUN, :] = kv_all[pl.ds(row, RUN), :]
        value_win[r, j * RUN : (j + 1) * RUN, :] = kv_all[pl.ds(row + tok_rows, RUN), :]
    return place_run, rows


def weights_of(doc_lengths, place_run, keys, q_rows, reach, heads):
    count = q_rows.shape[0]
    scaling = math.log2(math.e) / math.sqrt(keys.shape[1])
    lane = lax.broadcasted_iota(jnp.int32, (1, count), 1)
    q_off = lax.div(lax.rem(lane, RUN * heads), heads)
    q_pos = place_run * RUN + q_off
    doc_start = jnp.zeros_like(q_pos)
    doc_end = jnp.int32(0)
    for d in range(doc_lengths.shape[0]):
        doc_end = doc_end + doc_lengths[d]
        doc_start = jnp.where(doc_end <= q_pos, doc_end, doc_start)
    doc_start = doc_start - (place_run - (reach - 1)) * RUN
    scores = contract(keys, q_rows, 1, 1)
    early = (reach - 1) * RUN
    k_early = lax.broadcasted_iota(jnp.int32, (early, count), 0)
    k_own = lax.broadcasted_iota(jnp.int32, (RUN, count), 0)
    scores = jnp.concatenate(
        [
            jnp.where(k_early >= doc_start, scores[:early], NEGATIVE),
            jnp.where((k_own + early >= doc_start) & (k_own <= q_off), scores[early:], NEGATIVE),
        ],
        axis=0,
    )
    top = jnp.max(scores, axis=0, keepdims=True)
    raw = jnp.exp2((scores - top) * scaling)
    return raw, 1.0 / jnp.sum(raw, axis=0, keepdims=True)


def score_gradients(raw, one_over, values, g_rows):
    weights = raw * one_over
    grad_weights = contract(values, g_rows, 1, 1)
    row_inner = jnp.sum(weights * grad_weights, axis=0, keepdims=True)
    return weights, (weights * (grad_weights - row_inner)).astype(jnp.bfloat16)


def load_blocks(me, listed, blocks, kv_all):
    rows = min(block.shape[0] for block in blocks)
    for ks, block in zip(listed, blocks):
        for i, k in enumerate(ks):
            owner = lax.bitwise_xor(me, k)
            kv_all[pl.ds(pl.multiple_of(owner * rows, rows), rows), :] = block[i * rows : (i + 1) * rows, :]


def terms_kernel(listed, heads, reach, balance_in, docs_in, q_own, g_own, q_other, g_other, *refs):
    n_ctx, n_blocks = sum(len(ks) for ks in listed), len(listed)
    blocks, outs, scratch = refs[:n_blocks], refs[n_blocks : n_blocks + n_ctx], refs[n_blocks + n_ctx :]
    qg_all, kv_all, key_win, value_win, terms, *lists = scratch
    me, head = lax.axis_index("ctx"), lax.axis_index("head")
    both, width = min(block.shape[0] for block in blocks), blocks[0].shape[1]
    tok_rows = both // 2
    runs_here = tok_rows // RUN
    run_rows = RUN * heads
    copies = start_lists(balance_in, docs_in, lists)
    load_blocks(me, listed, blocks, kv_all)
    for sources, part in (((q_own, g_own), head), ((q_other, g_other), 1 - head)):
        at = pl.ds(pl.multiple_of(part * run_rows, run_rows), run_rows)
        for w, source in enumerate(sources):
            for r in range(runs_here):
                qg_all[w, r, at, :] = source[r * run_rows : (r + 1) * run_rows, :]
    terms[...] = jnp.zeros_like(terms)
    finish_lists(copies, lists)

    for r in range(runs_here):
        place_run, rows = run_window(me, lists, kv_all, key_win, value_win, r, reach, runs_here, tok_rows)
        q_rows, g_rows = qg_all[0, r], qg_all[1, r]
        raw, one_over = weights_of(lists[1], place_run, key_win[r], q_rows, reach, heads)
        weights, grad_scores = score_gradients(raw, one_over, value_win[r], g_rows)
        value_part = contract(weights.astype(jnp.bfloat16), g_rows, 1, 0)
        key_part = contract(grad_scores, q_rows, 1, 0) * (1.0 / math.sqrt(width))
        for j, row in enumerate(rows):
            part = slice(j * RUN, (j + 1) * RUN)
            terms[pl.ds(row, RUN), :] += key_part[part, :]
            terms[pl.ds(row + tok_rows, RUN), :] += value_part[part, :]

    for k in range(n_ctx):
        owner = lax.bitwise_xor(me, k)
        at = pl.ds(pl.multiple_of(owner * both, both), both)
        outs[k][...] = terms[at, :].astype(outs[k].dtype)


def gradient_terms(balance, doc_lengths, own, other, blocks, heads, reach):
    listed, blocks = zip(*blocks)
    n_ctx = sum(len(ks) for ks in listed)
    both, width = min(block.shape[0] for block in blocks), blocks[0].shape[1]
    tok_rows = both // 2
    runs_here = tok_rows // RUN
    kept = [k for k in range(n_ctx) if k in (0, 4) or 8 <= k < n_ctx // 2 or k < min(8, n_ctx // 2) and n_ctx > 8]
    outs = [
        jax.ShapeDtypeStruct((both, width), jnp.float32 if k in kept else jnp.bfloat16) for k in range(n_ctx)
    ]
    return pl.pallas_call(
        functools.partial(terms_kernel, listed, heads, reach),
        out_shape=outs,
        in_specs=[ANY] * 2 + [VMEM] * (4 + len(blocks)),
        out_specs=[VMEM] * n_ctx,
        scratch_shapes=[
            pltpu.VMEM((2, runs_here, 2 * RUN * heads, width), jnp.bfloat16),
            pltpu.VMEM((n_ctx * both, width), jnp.bfloat16),
            pltpu.VMEM((runs_here, reach * RUN, width), jnp.bfloat16),
            pltpu.VMEM((runs_here, reach * RUN, width), jnp.bfloat16),
            pltpu.VMEM((n_ctx * both, width), jnp.float32),
            pltpu.SMEM(balance.shape, jnp.int32),
            pltpu.SMEM(doc_lengths.shape, jnp.int32),
            pltpu.SMEM((balance.shape[0] // RUN,), jnp.int32),
            pltpu.SemaphoreType.DMA((2,)),
        ],
        compiler_params=limit(balance.shape[0]),
    )(balance, doc_lengths, *own, *other, *blocks)


def rows_kernel(n_after, listed, heads, reach, balance_in, docs_in, q_own, g_own, *refs):
    refs = refs[n_after:]
    n_blocks = len(listed)
    blocks, (att_out, qg_out), scratch = refs[:n_blocks], refs[n_blocks : n_blocks + 2], refs[n_blocks + 2 :]
    kv_all, key_win, value_win, att_buf, grad_buf, out_sem, *lists = scratch
    me = lax.axis_index("ctx")
    both, width = min(block.shape[0] for block in blocks), blocks[0].shape[1]
    tok_rows = both // 2
    runs_here = tok_rows // RUN
    run_rows = RUN * heads

    copies = start_lists(balance_in, docs_in, lists)
    load_blocks(me, listed, blocks, kv_all)
    finish_lists(copies, lists)

    out_copies = []
    for r in range(runs_here):
        place_run, _ = run_window(me, lists, kv_all, key_win, value_win, r, reach, runs_here, tok_rows)
        here = slice(r * run_rows, (r + 1) * run_rows)
        q_rows = q_own[here, :]
        g_rows = g_own[here, :]
        raw, one_over = weights_of(lists[1], place_run, key_win[r], q_rows, reach, heads)
        attended = contract(value_win[r], raw.astype(jnp.bfloat16), 0, 0) * one_over
        att_buf[here, :] = attended.T.astype(jnp.bfloat16)
        _, grad_scores = score_gradients(raw, one_over, value_win[r], g_rows)
        query_part = contract(key_win[r], grad_scores, 0, 0) * (1.0 / math.sqrt(width))
        grad_buf[here, :] = query_part.T.astype(jnp.bfloat16)
        for i, (source, out) in enumerate(((att_buf, att_out), (grad_buf, qg_out))):
            at = pl.ds(r * run_rows, run_rows)
            out_copies.append(pltpu.make_async_copy(source.at[at], out.at[at], out_sem.at[2 * r + i]))
            out_copies[-1].start()
    for copy in out_copies:
        copy.wait()


def query_side(balance, doc_lengths, own, after, blocks, heads, reach):
    listed, blocks = zip(*blocks)
    n_ctx = sum(len(ks) for ks in listed)
    both, width = min(block.shape[0] for block in blocks), blocks[0].shape[1]
    tok_rows = both // 2
    runs_here = tok_rows // RUN
    rows = own[0].shape[0]
    return pl.pallas_call(
        functools.partial(rows_kernel, len(after), listed, heads, reach),
        out_shape=[jax.ShapeDtypeStruct((rows, width), jnp.bfloat16)] * 2,
        in_specs=[ANY, ANY, VMEM, VMEM] + [ANY] * len(after) + [VMEM] * len(blocks),
        out_specs=[HBM] * 2,
        scratch_shapes=[
            pltpu.VMEM((n_ctx * both, width), jnp.bfloat16),
            pltpu.VMEM((runs_here, reach * RUN, width), jnp.bfloat16),
            pltpu.VMEM((runs_here, reach * RUN, width), jnp.bfloat16),
            pltpu.VMEM((rows, width), jnp.bfloat16),
            pltpu.VMEM((rows, width), jnp.bfloat16),
            pltpu.SemaphoreType.DMA((2 * runs_here,)),
            pltpu.SMEM(balance.shape, jnp.int32),
            pltpu.SMEM(doc_lengths.shape, jnp.int32),
            pltpu.SMEM((balance.shape[0] // RUN,), jnp.int32),
            pltpu.SemaphoreType.DMA((2,)),
        ],
        compiler_params=limit(balance.shape[0]),
    )(balance, doc_lengths, *own, *after, *blocks)


def body(n_ctx, n_head, queries, key_rows, value_rows, out_grad, doc_lengths, balance):
    tok_rows, heads, width = queries.shape
    seq_total = balance.shape[0]
    reach = seq_total // LONGEST_SHARE // RUN + 1

    def swap(array, k):
        return lax.ppermute(array, "ctx", [(i, i ^ k) for i in range(n_ctx)])

    own = [array.reshape(tok_rows * heads, width) for array in (queries, out_grad)]
    mine, balance, doc_lengths = pack(key_rows, value_rows, balance, doc_lengths)
    blocks = {0: mine}
    for k in (4, 1, 2, 3):
        if k not in MERGED:
            blocks[k] = swap(mine, k)
    other = [lax.ppermute(array, "head", [(i, n_head - 1 - i) for i in range(n_head)]) for array in own]
    merged = {}
    for k in FAR_ORDER:
        if k - 4 in MERGED:
            merged[k] = swap(join(mine, blocks[4], seq_total), k - 4)
        else:
            blocks[k] = swap(blocks[4], k - 4)
    blocks = [((k - 4, k), merged[k]) if k in merged else ((k,), blocks[k]) for k in BLOCK_ORDER if k not in MERGED]
    for bit, _ in high_bits(n_ctx):
        blocks += [(tuple(bit + k for k in ks), swap(block, bit)) for ks, block in blocks]
    terms = list(gradient_terms(balance, doc_lengths, own, other, blocks, heads, reach))

    for bit, below in reversed(high_bits(n_ctx)):
        for k in below:
            terms[k] = terms[k] + swap(terms[bit + k].astype(jnp.bfloat16), bit).astype(jnp.float32)
    far = terms[4]
    for k in BACK_ORDER:
        far = far + swap(terms[k].astype(jnp.bfloat16), k - 4).astype(jnp.float32)
    far = far.astype(jnp.bfloat16)
    total = terms[0]
    for k in SUM_ORDER:
        term = far if k == 4 else terms[k].astype(jnp.bfloat16)
        total = total + swap(term, k).astype(jnp.float32)
    after = [far]
    attended, query_grad = query_side(balance, doc_lengths, own, after, blocks, heads, reach)
    combined = total.astype(jnp.bfloat16)
    return (
        attended.reshape(tok_rows, heads, width),
        query_grad.reshape(tok_rows, heads, width),
        combined[:tok_rows],
        combined[tok_rows:],
    )


def solution(mesh):
    return jax.shard_map(
        functools.partial(body, mesh.shape["ctx"], mesh.shape["head"]),
        mesh=mesh,
        in_specs=(
            P(("seq", "ctx"), "head", None),
            P(("seq", "ctx"), None),
            P(("seq", "ctx"), None),
            P(("seq", "ctx"), "head", None),
            P("seq"),
            P("seq"),
        ),
        out_specs=(
            P(("seq", "ctx"), "head", None),
            P(("seq", "ctx"), "head", None),
            P(("seq", "ctx"), None),
            P(("seq", "ctx"), None),
        ),
        check_vma=False,
    )
```

```python
import functools
import math

import jax
import jax.numpy as jnp
from jax import lax
from jax.experimental import pallas as pl
from jax.experimental.pallas import tpu as pltpu
from jax.sharding import PartitionSpec as P

NEGATIVE = -1e30
RUN = 64
LONGEST_SHARE = 4

ANY = pl.BlockSpec(memory_space=pl.ANY)
VMEM = pl.BlockSpec(memory_space=pltpu.VMEM)
HBM = pl.BlockSpec(memory_space=pltpu.HBM)


def contract(a, b, dim_a, dim_b):
    return lax.dot_general(
        a, b, (((dim_a,), (dim_b,)), ((), ())), preferred_element_type=jnp.float32
    )


def limit(seq_total):
    return pltpu.CompilerParams(vmem_limit_bytes=(16 << 20) if seq_total <= 1024 else (56 << 20))


MERGED = (3,)
BLOCK_ORDER = (0, 1, 5, 2, 6, 4, 7, 3)
FAR_ORDER = (5, 6, 7)
BACK_ORDER = (7, 6, 5)
SUM_ORDER = (4, 3, 1, 2)


def high_bits(n_ctx):
    return [(1 << b, range(1 << b)) for b in range(3, n_ctx.bit_length() - 1)]


def join_kernel(first, second, out):
    rows = first.shape[0]
    out[:rows, :] = first[...]
    out[rows:, :] = second[...]


def join(first, second, seq_total):
    return pl.pallas_call(
        join_kernel,
        out_shape=jax.ShapeDtypeStruct((2 * first.shape[0], first.shape[1]), first.dtype),
        in_specs=[VMEM] * 2,
        out_specs=VMEM,
        compiler_params=limit(seq_total),
    )(first, second)


def pack_kernel(key_rows, value_rows, balance, doc_lengths, kv_out, balance_out, docs_out, sems):
    tok_rows = key_rows.shape[0]
    copies = [
        pltpu.make_async_copy(key_rows, kv_out.at[pl.ds(0, tok_rows)], sems.at[0]),
        pltpu.make_async_copy(value_rows, kv_out.at[pl.ds(tok_rows, tok_rows)], sems.at[1]),
        pltpu.make_async_copy(balance, balance_out, sems.at[2]),
        pltpu.make_async_copy(doc_lengths, docs_out, sems.at[3]),
    ]
    for copy in copies:
        copy.start()
    for copy in copies:
        copy.wait()


def pack(key_rows, value_rows, balance, doc_lengths):
    return pl.pallas_call(
        pack_kernel,
        out_shape=[
            jax.ShapeDtypeStruct((2 * key_rows.shape[0], key_rows.shape[1]), jnp.bfloat16),
            jax.ShapeDtypeStruct(balance.shape, jnp.int32),
            jax.ShapeDtypeStruct(doc_lengths.shape, jnp.int32),
        ],
        in_specs=[ANY] * 4,
        out_specs=[ANY] * 3,
        scratch_shapes=[pltpu.SemaphoreType.DMA((4,))],
        compiler_params=limit(balance.shape[0]),
    )(*[pltpu.with_memory_space_constraint(a, pltpu.HBM) for a in (key_rows, value_rows, balance, doc_lengths)])


def start_lists(balance_in, docs_in, lists):
    balance, doc_lengths, _, sems = lists
    copies = [
        pltpu.make_async_copy(balance_in, balance, sems.at[0]),
        pltpu.make_async_copy(docs_in, doc_lengths, sems.at[1]),
    ]
    for copy in copies:
        copy.start()
    return copies


def finish_lists(copies, lists):
    balance, _, slot_of, _ = lists
    runs = slot_of.shape[0]
    for copy in copies:
        copy.wait()

    def note(s, carry):
        slot_of[lax.shift_right_logical(balance[s * RUN], 6)] = s
        return carry

    lax.fori_loop(0, runs, note, 0, unroll=runs <= 16)


def run_window(me, lists, kv_all, key_win, value_win, r, reach, runs_here, tok_rows):
    balance, _, slot_of, _ = lists
    place_run = lax.shift_right_logical(balance[(me * runs_here + r) * RUN], 6)
    rows = []
    for j in range(reach):
        slot = slot_of[jnp.maximum(place_run - (reach - 1) + j, 0)]
        row = lax.div(slot, runs_here) * (2 * tok_rows) + lax.rem(slot, runs_here) * RUN
        row = pl.multiple_of(row, RUN)
        rows.append(row)
        key_win[r, j * RUN : (j + 1) * RUN, :] = kv_all[pl.ds(row, RUN), :]
        value_win[r, j * RUN : (j + 1) * RUN, :] = kv_all[pl.ds(row + tok_rows, RUN), :]
    return place_run, rows


def weights_of(doc_lengths, place_run, keys, q_rows, reach, heads):
    count = q_rows.shape[0]
    scaling = math.log2(math.e) / math.sqrt(keys.shape[1])
    lane = lax.broadcasted_iota(jnp.int32, (1, count), 1)
    q_off = lax.div(lax.rem(lane, RUN * heads), heads)
    q_pos = place_run * RUN + q_off
    doc_start = jnp.zeros_like(q_pos)
    doc_end = jnp.int32(0)
    for d in range(doc_lengths.shape[0]):
        doc_end = doc_end + doc_lengths[d]
        doc_start = jnp.where(doc_end <= q_pos, doc_end, doc_start)
    doc_start = doc_start - (place_run - (reach - 1)) * RUN
    scores = contract(keys, q_rows, 1, 1)
    early = (reach - 1) * RUN
    k_early = lax.broadcasted_iota(jnp.int32, (early, count), 0)
    k_own = lax.broadcasted_iota(jnp.int32, (RUN, count), 0)
    scores = jnp.concatenate(
        [
            jnp.where(k_early >= doc_start, scores[:early], NEGATIVE),
            jnp.where((k_own + early >= doc_start) & (k_own <= q_off), scores[early:], NEGATIVE),
        ],
        axis=0,
    )
    top = jnp.max(scores, axis=0, keepdims=True)
    raw = jnp.exp2((scores - top) * scaling)
    return raw, 1.0 / jnp.sum(raw, axis=0, keepdims=True)


def score_gradients(raw, one_over, values, g_rows):
    weights = raw * one_over
    grad_weights = contract(values, g_rows, 1, 1)
    row_inner = jnp.sum(weights * grad_weights, axis=0, keepdims=True)
    return weights, (weights * (grad_weights - row_inner)).astype(jnp.bfloat16)


def load_blocks(me, listed, blocks, kv_all):
    rows = min(block.shape[0] for block in blocks)
    for ks, block in zip(listed, blocks):
        for i, k in enumerate(ks):
            owner = lax.bitwise_xor(me, k)
            kv_all[pl.ds(pl.multiple_of(owner * rows, rows), rows), :] = block[i * rows : (i + 1) * rows, :]


def terms_kernel(listed, heads, reach, balance_in, docs_in, q_own, g_own, q_other, g_other, *refs):
    n_ctx, n_blocks = sum(len(ks) for ks in listed), len(listed)
    blocks, outs, scratch = refs[:n_blocks], refs[n_blocks : n_blocks + n_ctx], refs[n_blocks + n_ctx :]
    qg_all, kv_all, key_win, value_win, terms, *lists = scratch
    me, head = lax.axis_index("ctx"), lax.axis_index("head")
    both, width = min(block.shape[0] for block in blocks), blocks[0].shape[1]
    tok_rows = both // 2
    runs_here = tok_rows // RUN
    run_rows = RUN * heads
    copies = start_lists(balance_in, docs_in, lists)
    load_blocks(me, listed, blocks, kv_all)
    for sources, part in (((q_own, g_own), head), ((q_other, g_other), 1 - head)):
        at = pl.ds(pl.multiple_of(part * run_rows, run_rows), run_rows)
        for w, source in enumerate(sources):
            for r in range(runs_here):
                qg_all[w, r, at, :] = source[r * run_rows : (r + 1) * run_rows, :]
    terms[...] = jnp.zeros_like(terms)
    finish_lists(copies, lists)

    for r in range(runs_here):
        place_run, rows = run_window(me, lists, kv_all, key_win, value_win, r, reach, runs_here, tok_rows)
        q_rows, g_rows = qg_all[0, r], qg_all[1, r]
        raw, one_over = weights_of(lists[1], place_run, key_win[r], q_rows, reach, heads)
        weights, grad_scores = score_gradients(raw, one_over, value_win[r], g_rows)
        value_part = contract(weights.astype(jnp.bfloat16), g_rows, 1, 0)
        key_part = contract(grad_scores, q_rows, 1, 0) * (1.0 / math.sqrt(width))
        for j, row in enumerate(rows):
            part = slice(j * RUN, (j + 1) * RUN)
            terms[pl.ds(row, RUN), :] += key_part[part, :]
            terms[pl.ds(row + tok_rows, RUN), :] += value_part[part, :]

    for k in range(n_ctx):
        owner = lax.bitwise_xor(me, k)
        at = pl.ds(pl.multiple_of(owner * both, both), both)
        outs[k][...] = terms[at, :].astype(outs[k].dtype)


def gradient_terms(balance, doc_lengths, own, other, blocks, heads, reach):
    listed, blocks = zip(*blocks)
    n_ctx = sum(len(ks) for ks in listed)
    both, width = min(block.shape[0] for block in blocks), blocks[0].shape[1]
    tok_rows = both // 2
    runs_here = tok_rows // RUN
    kept = [k for k in range(n_ctx) if k in (0, 4) or 8 <= k < n_ctx // 2 or k < min(8, n_ctx // 2) and n_ctx > 8]
    outs = [
        jax.ShapeDtypeStruct((both, width), jnp.float32 if k in kept else jnp.bfloat16) for k in range(n_ctx)
    ]
    return pl.pallas_call(
        functools.partial(terms_kernel, listed, heads, reach),
        out_shape=outs,
        in_specs=[ANY] * 2 + [VMEM] * (4 + len(blocks)),
        out_specs=[VMEM] * n_ctx,
        scratch_shapes=[
            pltpu.VMEM((2, runs_here, 2 * RUN * heads, width), jnp.bfloat16),
            pltpu.VMEM((n_ctx * both, width), jnp.bfloat16),
            pltpu.VMEM((runs_here, reach * RUN, width), jnp.bfloat16),
            pltpu.VMEM((runs_here, reach * RUN, width), jnp.bfloat16),
            pltpu.VMEM((n_ctx * both, width), jnp.float32),
            pltpu.SMEM(balance.shape, jnp.int32),
            pltpu.SMEM(doc_lengths.shape, jnp.int32),
            pltpu.SMEM((balance.shape[0] // RUN,), jnp.int32),
            pltpu.SemaphoreType.DMA((2,)),
        ],
        compiler_params=limit(balance.shape[0]),
    )(balance, doc_lengths, *own, *other, *blocks)


def rows_kernel(n_after, listed, heads, reach, balance_in, docs_in, q_own, g_own, *refs):
    refs = refs[n_after:]
    n_blocks = len(listed)
    blocks, (att_out, qg_out), scratch = refs[:n_blocks], refs[n_blocks : n_blocks + 2], refs[n_blocks + 2 :]
    kv_all, key_win, value_win, att_buf, grad_buf, out_sem, *lists = scratch
    me = lax.axis_index("ctx")
    both, width = min(block.shape[0] for block in blocks), blocks[0].shape[1]
    tok_rows = both // 2
    runs_here = tok_rows // RUN
    run_rows = RUN * heads

    copies = start_lists(balance_in, docs_in, lists)
    load_blocks(me, listed, blocks, kv_all)
    finish_lists(copies, lists)

    out_copies = []
    for r in range(runs_here):
        place_run, _ = run_window(me, lists, kv_all, key_win, value_win, r, reach, runs_here, tok_rows)
        here = slice(r * run_rows, (r + 1) * run_rows)
        q_rows = q_own[here, :]
        g_rows = g_own[here, :]
        raw, one_over = weights_of(lists[1], place_run, key_win[r], q_rows, reach, heads)
        attended = contract(value_win[r], raw.astype(jnp.bfloat16), 0, 0) * one_over
        att_buf[here, :] = attended.T.astype(jnp.bfloat16)
        _, grad_scores = score_gradients(raw, one_over, value_win[r], g_rows)
        query_part = contract(key_win[r], grad_scores, 0, 0) * (1.0 / math.sqrt(width))
        grad_buf[here, :] = query_part.T.astype(jnp.bfloat16)
        for i, (source, out) in enumerate(((att_buf, att_out), (grad_buf, qg_out))):
            at = pl.ds(r * run_rows, run_rows)
            out_copies.append(pltpu.make_async_copy(source.at[at], out.at[at], out_sem.at[2 * r + i]))
            out_copies[-1].start()
    for copy in out_copies:
        copy.wait()


def query_side(balance, doc_lengths, own, after, blocks, heads, reach):
    listed, blocks = zip(*blocks)
    n_ctx = sum(len(ks) for ks in listed)
    both, width = min(block.shape[0] for block in blocks), blocks[0].shape[1]
    tok_rows = both // 2
    runs_here = tok_rows // RUN
    rows = own[0].shape[0]
    return pl.pallas_call(
        functools.partial(rows_kernel, len(after), listed, heads, reach),
        out_shape=[jax.ShapeDtypeStruct((rows, width), jnp.bfloat16)] * 2,
        in_specs=[ANY, ANY, VMEM, VMEM] + [ANY] * len(after) + [VMEM] * len(blocks),
        out_specs=[HBM] * 2,
        scratch_shapes=[
            pltpu.VMEM((n_ctx * both, width), jnp.bfloat16),
            pltpu.VMEM((runs_here, reach * RUN, width), jnp.bfloat16),
            pltpu.VMEM((runs_here, reach * RUN, width), jnp.bfloat16),
            pltpu.VMEM((rows, width), jnp.bfloat16),
            pltpu.VMEM((rows, width), jnp.bfloat16),
            pltpu.SemaphoreType.DMA((2 * runs_here,)),
            pltpu.SMEM(balance.shape, jnp.int32),
            pltpu.SMEM(doc_lengths.shape, jnp.int32),
            pltpu.SMEM((balance.shape[0] // RUN,), jnp.int32),
            pltpu.SemaphoreType.DMA((2,)),
        ],
        compiler_params=limit(balance.shape[0]),
    )(balance, doc_lengths, *own, *after, *blocks)


def body(n_ctx, n_head, queries, key_rows, value_rows, out_grad, doc_lengths, balance):
    tok_rows, heads, width = queries.shape
    seq_total = balance.shape[0]
    reach = seq_total // LONGEST_SHARE // RUN + 1

    def swap(array, k):
        return lax.ppermute(array, "ctx", [(i, i ^ k) for i in range(n_ctx)])

    own = [array.reshape(tok_rows * heads, width) for array in (queries, out_grad)]
    mine, balance, doc_lengths = pack(key_rows, value_rows, balance, doc_lengths)
    blocks = {0: mine}
    for k in (4, 1, 2, 3):
        if k not in MERGED:
            blocks[k] = swap(mine, k)
    other = [lax.ppermute(array, "head", [(i, n_head - 1 - i) for i in range(n_head)]) for array in own]
    merged = {}
    for k in FAR_ORDER:
        if k - 4 in MERGED:
            merged[k] = swap(join(mine, blocks[4], seq_total), k - 4)
        else:
            blocks[k] = swap(blocks[4], k - 4)
    blocks = [((k - 4, k), merged[k]) if k in merged else ((k,), blocks[k]) for k in BLOCK_ORDER if k not in MERGED]
    for bit, _ in high_bits(n_ctx):
        blocks += [(tuple(bit + k for k in ks), swap(block, bit)) for ks, block in blocks]
    terms = list(gradient_terms(balance, doc_lengths, own, other, blocks, heads, reach))

    for bit, below in reversed(high_bits(n_ctx)):
        for k in below:
            terms[k] = terms[k] + swap(terms[bit + k].astype(jnp.bfloat16), bit).astype(jnp.float32)
    far = terms[4]
    for k in BACK_ORDER:
        far = far + swap(terms[k].astype(jnp.bfloat16), k - 4).astype(jnp.float32)
    far = far.astype(jnp.bfloat16)
    total = terms[0]
    for k in SUM_ORDER:
        term = far if k == 4 else terms[k].astype(jnp.bfloat16)
        total = total + swap(term, k).astype(jnp.float32)
    after = [far]
    attended, query_grad = query_side(balance, doc_lengths, own, after, blocks, heads, reach)
    combined = total.astype(jnp.bfloat16)
    return (
        attended.reshape(tok_rows, heads, width),
        query_grad.reshape(tok_rows, heads, width),
        combined[:tok_rows],
        combined[tok_rows:],
    )


def solution(mesh):
    return jax.shard_map(
        functools.partial(body, mesh.shape["ctx"], mesh.shape["head"]),
        mesh=mesh,
        in_specs=(
            P(("seq", "ctx"), "head", None),
            P(("seq", "ctx"), None),
            P(("seq", "ctx"), None),
            P(("seq", "ctx"), "head", None),
            P("seq"),
            P("seq"),
        ),
        out_specs=(
            P(("seq", "ctx"), "head", None),
            P(("seq", "ctx"), "head", None),
            P(("seq", "ctx"), None),
            P(("seq", "ctx"), None),
        ),
        check_vma=False,
    )
```

```python
import functools
import math

import jax
import jax.numpy as jnp
from jax import lax
from jax.experimental import pallas as pl
from jax.experimental.pallas import tpu as pltpu
from jax.sharding import PartitionSpec as P

NEGATIVE = -1e30
RUN = 64
LONGEST_SHARE = 4

ANY = pl.BlockSpec(memory_space=pl.ANY)
VMEM = pl.BlockSpec(memory_space=pltpu.VMEM)
HBM = pl.BlockSpec(memory_space=pltpu.HBM)


def contract(a, b, dim_a, dim_b):
    return lax.dot_general(
        a, b, (((dim_a,), (dim_b,)), ((), ())), preferred_element_type=jnp.float32
    )


def limit(seq_total):
    return pltpu.CompilerParams(vmem_limit_bytes=(16 << 20) if seq_total <= 1024 else (56 << 20))


MERGED = (3,)
BLOCK_ORDER = (0, 6, 4, 1, 2, 5, 3, 7)
FAR_ORDER = (5, 6, 7)
BACK_ORDER = (7, 6, 5)
SUM_ORDER = (1, 2, 3, 4)


def high_bits(n_ctx):
    return [(1 << b, range(1 << b)) for b in range(3, n_ctx.bit_length() - 1)]


def join_kernel(first, second, out):
    rows = first.shape[0]
    out[:rows, :] = first[...]
    out[rows:, :] = second[...]


def join(first, second, seq_total):
    return pl.pallas_call(
        join_kernel,
        out_shape=jax.ShapeDtypeStruct((2 * first.shape[0], first.shape[1]), first.dtype),
        in_specs=[VMEM] * 2,
        out_specs=VMEM,
        compiler_params=limit(seq_total),
    )(first, second)


def pack_kernel(key_rows, value_rows, balance, doc_lengths, kv_out, balance_out, docs_out, sems):
    tok_rows = key_rows.shape[0]
    copies = [
        pltpu.make_async_copy(key_rows, kv_out.at[pl.ds(0, tok_rows)], sems.at[0]),
        pltpu.make_async_copy(value_rows, kv_out.at[pl.ds(tok_rows, tok_rows)], sems.at[1]),
        pltpu.make_async_copy(balance, balance_out, sems.at[2]),
        pltpu.make_async_copy(doc_lengths, docs_out, sems.at[3]),
    ]
    for copy in copies:
        copy.start()
    for copy in copies:
        copy.wait()


def pack(key_rows, value_rows, balance, doc_lengths):
    return pl.pallas_call(
        pack_kernel,
        out_shape=[
            jax.ShapeDtypeStruct((2 * key_rows.shape[0], key_rows.shape[1]), jnp.bfloat16),
            jax.ShapeDtypeStruct(balance.shape, jnp.int32),
            jax.ShapeDtypeStruct(doc_lengths.shape, jnp.int32),
        ],
        in_specs=[ANY] * 4,
        out_specs=[ANY] * 3,
        scratch_shapes=[pltpu.SemaphoreType.DMA((4,))],
        compiler_params=limit(balance.shape[0]),
    )(*[pltpu.with_memory_space_constraint(a, pltpu.HBM) for a in (key_rows, value_rows, balance, doc_lengths)])


def start_lists(balance_in, docs_in, lists):
    balance, doc_lengths, _, sems = lists
    copies = [
        pltpu.make_async_copy(balance_in, balance, sems.at[0]),
        pltpu.make_async_copy(docs_in, doc_lengths, sems.at[1]),
    ]
    for copy in copies:
        copy.start()
    return copies


def finish_lists(copies, lists):
    balance, _, slot_of, _ = lists
    runs = slot_of.shape[0]
    for copy in copies:
        copy.wait()

    def note(s, carry):
        slot_of[lax.shift_right_logical(balance[s * RUN], 6)] = s
        return carry

    lax.fori_loop(0, runs, note, 0, unroll=runs <= 16)


def run_window(me, lists, kv_all, key_win, value_win, r, reach, runs_here, tok_rows):
    balance, _, slot_of, _ = lists
    place_run = lax.shift_right_logical(balance[(me * runs_here + r) * RUN], 6)
    rows = []
    for j in range(reach):
        slot = slot_of[jnp.maximum(place_run - (reach - 1) + j, 0)]
        row = lax.div(slot, runs_here) * (2 * tok_rows) + lax.rem(slot, runs_here) * RUN
        row = pl.multiple_of(row, RUN)
        rows.append(row)
        key_win[r, j * RUN : (j + 1) * RUN, :] = kv_all[pl.ds(row, RUN), :]
        value_win[r, j * RUN : (j + 1) * RUN, :] = kv_all[pl.ds(row + tok_rows, RUN), :]
    return place_run, rows


def weights_of(doc_lengths, place_run, keys, q_rows, reach, heads):
    count = q_rows.shape[0]
    scaling = math.log2(math.e) / math.sqrt(keys.shape[1])
    lane = lax.broadcasted_iota(jnp.int32, (1, count), 1)
    q_off = lax.div(lax.rem(lane, RUN * heads), heads)
    q_pos = place_run * RUN + q_off
    doc_start = jnp.zeros_like(q_pos)
    doc_end = jnp.int32(0)
    for d in range(doc_lengths.shape[0]):
        doc_end = doc_end + doc_lengths[d]
        doc_start = jnp.where(doc_end <= q_pos, doc_end, doc_start)
    doc_start = doc_start - (place_run - (reach - 1)) * RUN
    scores = contract(keys, q_rows, 1, 1)
    early = (reach - 1) * RUN
    k_early = lax.broadcasted_iota(jnp.int32, (early, count), 0)
    k_own = lax.broadcasted_iota(jnp.int32, (RUN, count), 0)
    scores = jnp.concatenate(
        [
            jnp.where(k_early >= doc_start, scores[:early], NEGATIVE),
            jnp.where((k_own + early >= doc_start) & (k_own <= q_off), scores[early:], NEGATIVE),
        ],
        axis=0,
    )
    top = jnp.max(scores, axis=0, keepdims=True)
    raw = jnp.exp2((scores - top) * scaling)
    return raw, 1.0 / jnp.sum(raw, axis=0, keepdims=True)


def score_gradients(raw, one_over, values, g_rows):
    weights = raw * one_over
    grad_weights = contract(values, g_rows, 1, 1)
    row_inner = jnp.sum(weights * grad_weights, axis=0, keepdims=True)
    return weights, (weights * (grad_weights - row_inner)).astype(jnp.bfloat16)


def load_blocks(me, listed, blocks, kv_all):
    rows = min(block.shape[0] for block in blocks)
    for ks, block in zip(listed, blocks):
        for i, k in enumerate(ks):
            owner = lax.bitwise_xor(me, k)
            kv_all[pl.ds(pl.multiple_of(owner * rows, rows), rows), :] = block[i * rows : (i + 1) * rows, :]


def terms_kernel(listed, heads, reach, balance_in, docs_in, q_own, g_own, q_other, g_other, *refs):
    n_ctx, n_blocks = sum(len(ks) for ks in listed), len(listed)
    blocks, outs, scratch = refs[:n_blocks], refs[n_blocks : n_blocks + n_ctx], refs[n_blocks + n_ctx :]
    qg_all, kv_all, key_win, value_win, terms, *lists = scratch
    me, head = lax.axis_index("ctx"), lax.axis_index("head")
    both, width = min(block.shape[0] for block in blocks), blocks[0].shape[1]
    tok_rows = both // 2
    runs_here = tok_rows // RUN
    run_rows = RUN * heads
    copies = start_lists(balance_in, docs_in, lists)
    load_blocks(me, listed, blocks, kv_all)
    for sources, part in (((q_own, g_own), head), ((q_other, g_other), 1 - head)):
        at = pl.ds(pl.multiple_of(part * run_rows, run_rows), run_rows)
        for w, source in enumerate(sources):
            for r in range(runs_here):
                qg_all[w, r, at, :] = source[r * run_rows : (r + 1) * run_rows, :]
    terms[...] = jnp.zeros_like(terms)
    finish_lists(copies, lists)

    for r in range(runs_here):
        place_run, rows = run_window(me, lists, kv_all, key_win, value_win, r, reach, runs_here, tok_rows)
        q_rows, g_rows = qg_all[0, r], qg_all[1, r]
        raw, one_over = weights_of(lists[1], place_run, key_win[r], q_rows, reach, heads)
        weights, grad_scores = score_gradients(raw, one_over, value_win[r], g_rows)
        value_part = contract(weights.astype(jnp.bfloat16), g_rows, 1, 0)
        key_part = contract(grad_scores, q_rows, 1, 0) * (1.0 / math.sqrt(width))
        for j, row in enumerate(rows):
            part = slice(j * RUN, (j + 1) * RUN)
            terms[pl.ds(row, RUN), :] += key_part[part, :]
            terms[pl.ds(row + tok_rows, RUN), :] += value_part[part, :]

    for k in range(n_ctx):
        owner = lax.bitwise_xor(me, k)
        at = pl.ds(pl.multiple_of(owner * both, both), both)
        outs[k][...] = terms[at, :].astype(outs[k].dtype)


def gradient_terms(balance, doc_lengths, own, other, blocks, heads, reach):
    listed, blocks = zip(*blocks)
    n_ctx = sum(len(ks) for ks in listed)
    both, width = min(block.shape[0] for block in blocks), blocks[0].shape[1]
    tok_rows = both // 2
    runs_here = tok_rows // RUN
    kept = [k for k in range(n_ctx) if k in (0, 4) or 8 <= k < n_ctx // 2 or k < min(8, n_ctx // 2) and n_ctx > 8]
    outs = [
        jax.ShapeDtypeStruct((both, width), jnp.float32 if k in kept else jnp.bfloat16) for k in range(n_ctx)
    ]
    return pl.pallas_call(
        functools.partial(terms_kernel, listed, heads, reach),
        out_shape=outs,
        in_specs=[ANY] * 2 + [VMEM] * (4 + len(blocks)),
        out_specs=[VMEM] * n_ctx,
        scratch_shapes=[
            pltpu.VMEM((2, runs_here, 2 * RUN * heads, width), jnp.bfloat16),
            pltpu.VMEM((n_ctx * both, width), jnp.bfloat16),
            pltpu.VMEM((runs_here, reach * RUN, width), jnp.bfloat16),
            pltpu.VMEM((runs_here, reach * RUN, width), jnp.bfloat16),
            pltpu.VMEM((n_ctx * both, width), jnp.float32),
            pltpu.SMEM(balance.shape, jnp.int32),
            pltpu.SMEM(doc_lengths.shape, jnp.int32),
            pltpu.SMEM((balance.shape[0] // RUN,), jnp.int32),
            pltpu.SemaphoreType.DMA((2,)),
        ],
        compiler_params=limit(balance.shape[0]),
    )(balance, doc_lengths, *own, *other, *blocks)


def rows_kernel(n_after, listed, heads, reach, balance_in, docs_in, q_own, g_own, *refs):
    refs = refs[n_after:]
    n_blocks = len(listed)
    blocks, (att_out, qg_out), scratch = refs[:n_blocks], refs[n_blocks : n_blocks + 2], refs[n_blocks + 2 :]
    kv_all, key_win, value_win, att_buf, grad_buf, out_sem, *lists = scratch
    me = lax.axis_index("ctx")
    both, width = min(block.shape[0] for block in blocks), blocks[0].shape[1]
    tok_rows = both // 2
    runs_here = tok_rows // RUN
    run_rows = RUN * heads

    copies = start_lists(balance_in, docs_in, lists)
    load_blocks(me, listed, blocks, kv_all)
    finish_lists(copies, lists)

    out_copies = []
    for r in range(runs_here):
        place_run, _ = run_window(me, lists, kv_all, key_win, value_win, r, reach, runs_here, tok_rows)
        here = slice(r * run_rows, (r + 1) * run_rows)
        q_rows = q_own[here, :]
        g_rows = g_own[here, :]
        raw, one_over = weights_of(lists[1], place_run, key_win[r], q_rows, reach, heads)
        attended = contract(value_win[r], raw.astype(jnp.bfloat16), 0, 0) * one_over
        att_buf[here, :] = attended.T.astype(jnp.bfloat16)
        _, grad_scores = score_gradients(raw, one_over, value_win[r], g_rows)
        query_part = contract(key_win[r], grad_scores, 0, 0) * (1.0 / math.sqrt(width))
        grad_buf[here, :] = query_part.T.astype(jnp.bfloat16)
        for i, (source, out) in enumerate(((att_buf, att_out), (grad_buf, qg_out))):
            at = pl.ds(r * run_rows, run_rows)
            out_copies.append(pltpu.make_async_copy(source.at[at], out.at[at], out_sem.at[2 * r + i]))
            out_copies[-1].start()
    for copy in out_copies:
        copy.wait()


def query_side(balance, doc_lengths, own, after, blocks, heads, reach):
    listed, blocks = zip(*blocks)
    n_ctx = sum(len(ks) for ks in listed)
    both, width = min(block.shape[0] for block in blocks), blocks[0].shape[1]
    tok_rows = both // 2
    runs_here = tok_rows // RUN
    rows = own[0].shape[0]
    return pl.pallas_call(
        functools.partial(rows_kernel, len(after), listed, heads, reach),
        out_shape=[jax.ShapeDtypeStruct((rows, width), jnp.bfloat16)] * 2,
        in_specs=[ANY, ANY, VMEM, VMEM] + [ANY] * len(after) + [VMEM] * len(blocks),
        out_specs=[HBM] * 2,
        scratch_shapes=[
            pltpu.VMEM((n_ctx * both, width), jnp.bfloat16),
            pltpu.VMEM((runs_here, reach * RUN, width), jnp.bfloat16),
            pltpu.VMEM((runs_here, reach * RUN, width), jnp.bfloat16),
            pltpu.VMEM((rows, width), jnp.bfloat16),
            pltpu.VMEM((rows, width), jnp.bfloat16),
            pltpu.SemaphoreType.DMA((2 * runs_here,)),
            pltpu.SMEM(balance.shape, jnp.int32),
            pltpu.SMEM(doc_lengths.shape, jnp.int32),
            pltpu.SMEM((balance.shape[0] // RUN,), jnp.int32),
            pltpu.SemaphoreType.DMA((2,)),
        ],
        compiler_params=limit(balance.shape[0]),
    )(balance, doc_lengths, *own, *after, *blocks)


def body(n_ctx, n_head, queries, key_rows, value_rows, out_grad, doc_lengths, balance):
    tok_rows, heads, width = queries.shape
    seq_total = balance.shape[0]
    reach = seq_total // LONGEST_SHARE // RUN + 1

    def swap(array, k):
        return lax.ppermute(array, "ctx", [(i, i ^ k) for i in range(n_ctx)])

    own = [array.reshape(tok_rows * heads, width) for array in (queries, out_grad)]
    mine, balance, doc_lengths = pack(key_rows, value_rows, balance, doc_lengths)
    blocks = {0: mine}
    for k in (4, 1, 2, 3):
        if k not in MERGED:
            blocks[k] = swap(mine, k)
    other = [lax.ppermute(array, "head", [(i, n_head - 1 - i) for i in range(n_head)]) for array in own]
    merged = {}
    for k in FAR_ORDER:
        if k - 4 in MERGED:
            merged[k] = swap(join(mine, blocks[4], seq_total), k - 4)
        else:
            blocks[k] = swap(blocks[4], k - 4)
    blocks = [((k - 4, k), merged[k]) if k in merged else ((k,), blocks[k]) for k in BLOCK_ORDER if k not in MERGED]
    for bit, _ in high_bits(n_ctx):
        blocks += [(tuple(bit + k for k in ks), swap(block, bit)) for ks, block in blocks]
    terms = list(gradient_terms(balance, doc_lengths, own, other, blocks, heads, reach))

    for bit, below in reversed(high_bits(n_ctx)):
        for k in below:
            terms[k] = terms[k] + swap(terms[bit + k].astype(jnp.bfloat16), bit).astype(jnp.float32)
    far = terms[4]
    for k in BACK_ORDER:
        far = far + swap(terms[k].astype(jnp.bfloat16), k - 4).astype(jnp.float32)
    far = far.astype(jnp.bfloat16)
    total = terms[0]
    for k in SUM_ORDER:
        term = far if k == 4 else terms[k].astype(jnp.bfloat16)
        total = total + swap(term, k).astype(jnp.float32)
    after = [far]
    attended, query_grad = query_side(balance, doc_lengths, own, after, blocks, heads, reach)
    combined = total.astype(jnp.bfloat16)
    return (
        attended.reshape(tok_rows, heads, width),
        query_grad.reshape(tok_rows, heads, width),
        combined[:tok_rows],
        combined[tok_rows:],
    )


def solution(mesh):
    return jax.shard_map(
        functools.partial(body, mesh.shape["ctx"], mesh.shape["head"]),
        mesh=mesh,
        in_specs=(
            P(("seq", "ctx"), "head", None),
            P(("seq", "ctx"), None),
            P(("seq", "ctx"), None),
            P(("seq", "ctx"), "head", None),
            P("seq"),
            P("seq"),
        ),
        out_specs=(
            P(("seq", "ctx"), "head", None),
            P(("seq", "ctx"), "head", None),
            P(("seq", "ctx"), None),
            P(("seq", "ctx"), None),
        ),
        check_vma=False,
    )
```

```python
import functools
import math

import jax
import jax.numpy as jnp
from jax import lax
from jax.experimental import pallas as pl
from jax.experimental.pallas import tpu as pltpu
from jax.sharding import PartitionSpec as P

NEGATIVE = -1e30
RUN = 64
LONGEST_SHARE = 4

ANY = pl.BlockSpec(memory_space=pl.ANY)
VMEM = pl.BlockSpec(memory_space=pltpu.VMEM)
HBM = pl.BlockSpec(memory_space=pltpu.HBM)


def contract(a, b, dim_a, dim_b):
    return lax.dot_general(
        a, b, (((dim_a,), (dim_b,)), ((), ())), preferred_element_type=jnp.float32
    )


def limit(seq_total):
    return pltpu.CompilerParams(vmem_limit_bytes=(16 << 20) if seq_total <= 1024 else (56 << 20))


MERGED = (3,)
BLOCK_ORDER = (0, 6, 4, 1, 2, 5, 3, 7)
FAR_ORDER = (5, 6, 7)
BACK_ORDER = (7, 6, 5)
SUM_ORDER = (1, 2, 3, 4)


def high_bits(n_ctx):
    return [(1 << b, range(1 << b)) for b in range(3, n_ctx.bit_length() - 1)]


def join_kernel(first, second, out):
    rows = first.shape[0]
    out[:rows, :] = first[...]
    out[rows:, :] = second[...]


def join(first, second, seq_total):
    return pl.pallas_call(
        join_kernel,
        out_shape=jax.ShapeDtypeStruct((2 * first.shape[0], first.shape[1]), first.dtype),
        in_specs=[VMEM] * 2,
        out_specs=VMEM,
        compiler_params=limit(seq_total),
    )(first, second)


def pack_kernel(key_rows, value_rows, balance, doc_lengths, kv_out, balance_out, docs_out, sems):
    tok_rows = key_rows.shape[0]
    copies = [
        pltpu.make_async_copy(key_rows, kv_out.at[pl.ds(0, tok_rows)], sems.at[0]),
        pltpu.make_async_copy(value_rows, kv_out.at[pl.ds(tok_rows, tok_rows)], sems.at[1]),
        pltpu.make_async_copy(balance, balance_out, sems.at[2]),
        pltpu.make_async_copy(doc_lengths, docs_out, sems.at[3]),
    ]
    for copy in copies:
        copy.start()
    for copy in copies:
        copy.wait()


def pack(key_rows, value_rows, balance, doc_lengths):
    return pl.pallas_call(
        pack_kernel,
        out_shape=[
            jax.ShapeDtypeStruct((2 * key_rows.shape[0], key_rows.shape[1]), jnp.bfloat16),
            jax.ShapeDtypeStruct(balance.shape, jnp.int32),
            jax.ShapeDtypeStruct(doc_lengths.shape, jnp.int32),
        ],
        in_specs=[ANY] * 4,
        out_specs=[ANY] * 3,
        scratch_shapes=[pltpu.SemaphoreType.DMA((4,))],
        compiler_params=limit(balance.shape[0]),
    )(*[pltpu.with_memory_space_constraint(a, pltpu.HBM) for a in (key_rows, value_rows, balance, doc_lengths)])


def start_lists(balance_in, docs_in, lists):
    balance, doc_lengths, _, sems = lists
    copies = [
        pltpu.make_async_copy(balance_in, balance, sems.at[0]),
        pltpu.make_async_copy(docs_in, doc_lengths, sems.at[1]),
    ]
    for copy in copies:
        copy.start()
    return copies


def finish_lists(copies, lists):
    balance, _, slot_of, _ = lists
    runs = slot_of.shape[0]
    for copy in copies:
        copy.wait()

    def note(s, carry):
        slot_of[lax.shift_right_logical(balance[s * RUN], 6)] = s
        return carry

    lax.fori_loop(0, runs, note, 0, unroll=runs <= 16)


def run_window(me, lists, kv_all, key_win, value_win, r, reach, runs_here, tok_rows):
    balance, _, slot_of, _ = lists
    place_run = lax.shift_right_logical(balance[(me * runs_here + r) * RUN], 6)
    rows = []
    for j in range(reach):
        slot = slot_of[jnp.maximum(place_run - (reach - 1) + j, 0)]
        row = lax.div(slot, runs_here) * (2 * tok_rows) + lax.rem(slot, runs_here) * RUN
        row = pl.multiple_of(row, RUN)
        rows.append(row)
        key_win[r, j * RUN : (j + 1) * RUN, :] = kv_all[pl.ds(row, RUN), :]
        value_win[r, j * RUN : (j + 1) * RUN, :] = kv_all[pl.ds(row + tok_rows, RUN), :]
    return place_run, rows


def weights_of(doc_lengths, place_run, keys, q_rows, reach, heads):
    count = q_rows.shape[0]
    scaling = math.log2(math.e) / math.sqrt(keys.shape[1])
    lane = lax.broadcasted_iota(jnp.int32, (1, count), 1)
    q_off = lax.div(lax.rem(lane, RUN * heads), heads)
    q_pos = place_run * RUN + q_off
    doc_start = jnp.zeros_like(q_pos)
    doc_end = jnp.int32(0)
    for d in range(doc_lengths.shape[0]):
        doc_end = doc_end + doc_lengths[d]
        doc_start = jnp.where(doc_end <= q_pos, doc_end, doc_start)
    doc_start = doc_start - (place_run - (reach - 1)) * RUN
    scores = contract(keys, q_rows, 1, 1)
    early = (reach - 1) * RUN
    k_early = lax.broadcasted_iota(jnp.int32, (early, count), 0)
    k_own = lax.broadcasted_iota(jnp.int32, (RUN, count), 0)
    scores = jnp.concatenate(
        [
            jnp.where(k_early >= doc_start, scores[:early], NEGATIVE),
            jnp.where((k_own + early >= doc_start) & (k_own <= q_off), scores[early:], NEGATIVE),
        ],
        axis=0,
    )
    top = jnp.max(scores, axis=0, keepdims=True)
    raw = jnp.exp2((scores - top) * scaling)
    return raw, 1.0 / jnp.sum(raw, axis=0, keepdims=True)


def score_gradients(raw, one_over, values, g_rows):
    weights = raw * one_over
    grad_weights = contract(values, g_rows, 1, 1)
    row_inner = jnp.sum(weights * grad_weights, axis=0, keepdims=True)
    return weights, (weights * (grad_weights - row_inner)).astype(jnp.bfloat16)


def load_blocks(me, listed, blocks, kv_all):
    rows = min(block.shape[0] for block in blocks)
    for ks, block in zip(listed, blocks):
        for i, k in enumerate(ks):
            owner = lax.bitwise_xor(me, k)
            kv_all[pl.ds(pl.multiple_of(owner * rows, rows), rows), :] = block[i * rows : (i + 1) * rows, :]


def terms_kernel(listed, heads, reach, balance_in, docs_in, qg_all, *refs):
    n_ctx, n_blocks = sum(len(ks) for ks in listed), len(listed)
    blocks, outs, scratch = refs[:n_blocks], refs[n_blocks : n_blocks + n_ctx], refs[n_blocks + n_ctx :]
    kv_all, key_win, value_win, terms, *lists = scratch
    me = lax.axis_index("ctx")
    both, width = min(block.shape[0] for block in blocks), blocks[0].shape[1]
    tok_rows = both // 2
    runs_here = tok_rows // RUN
    run_rows = RUN * heads
    copies = start_lists(balance_in, docs_in, lists)
    load_blocks(me, listed, blocks, kv_all)
    terms[...] = jnp.zeros_like(terms)
    finish_lists(copies, lists)

    for r in range(runs_here):
        place_run, rows = run_window(me, lists, kv_all, key_win, value_win, r, reach, runs_here, tok_rows)
        q_rows, g_rows = qg_all[0, r], qg_all[1, r]
        raw, one_over = weights_of(lists[1], place_run, key_win[r], q_rows, reach, heads)
        weights, grad_scores = score_gradients(raw, one_over, value_win[r], g_rows)
        value_part = contract(weights.astype(jnp.bfloat16), g_rows, 1, 0)
        key_part = contract(grad_scores, q_rows, 1, 0) * (1.0 / math.sqrt(width))
        for j, row in enumerate(rows):
            part = slice(j * RUN, (j + 1) * RUN)
            terms[pl.ds(row, RUN), :] += key_part[part, :]
            terms[pl.ds(row + tok_rows, RUN), :] += value_part[part, :]

    for k in range(n_ctx):
        owner = lax.bitwise_xor(me, k)
        at = pl.ds(pl.multiple_of(owner * both, both), both)
        outs[k][...] = terms[at, :].astype(outs[k].dtype)


def order_kernel(run_rows, q_own, g_own, q_other, g_other, out):
    head = lax.axis_index("head")
    for sources, part in (((q_own, g_own), head), ((q_other, g_other), 1 - head)):
        at = pl.ds(pl.multiple_of(part * run_rows, run_rows), run_rows)
        for w, source in enumerate(sources):
            for r in range(out.shape[1]):
                out[w, r, at, :] = source[r * run_rows : (r + 1) * run_rows, :]


def order_heads(own, other, heads, seq_total):
    rows, width = own[0].shape
    run_rows = RUN * heads
    return pl.pallas_call(
        functools.partial(order_kernel, run_rows),
        out_shape=jax.ShapeDtypeStruct((2, rows // run_rows, 2 * run_rows, width), jnp.bfloat16),
        in_specs=[VMEM] * 4,
        out_specs=VMEM,
        compiler_params=limit(seq_total),
    )(*own, *other)


def gradient_terms(balance, doc_lengths, by_head, blocks, heads, reach):
    listed, blocks = zip(*blocks)
    n_ctx = sum(len(ks) for ks in listed)
    both, width = min(block.shape[0] for block in blocks), blocks[0].shape[1]
    tok_rows = both // 2
    runs_here = tok_rows // RUN
    kept = [k for k in range(n_ctx) if k in (0, 4) or 8 <= k < n_ctx // 2 or k < min(8, n_ctx // 2) and n_ctx > 8]
    outs = [
        jax.ShapeDtypeStruct((both, width), jnp.float32 if k in kept else jnp.bfloat16) for k in range(n_ctx)
    ]
    return pl.pallas_call(
        functools.partial(terms_kernel, listed, heads, reach),
        out_shape=outs,
        in_specs=[ANY] * 2 + [VMEM] * (1 + len(blocks)),
        out_specs=[VMEM] * n_ctx,
        scratch_shapes=[
            pltpu.VMEM((n_ctx * both, width), jnp.bfloat16),
            pltpu.VMEM((runs_here, reach * RUN, width), jnp.bfloat16),
            pltpu.VMEM((runs_here, reach * RUN, width), jnp.bfloat16),
            pltpu.VMEM((n_ctx * both, width), jnp.float32),
            pltpu.SMEM(balance.shape, jnp.int32),
            pltpu.SMEM(doc_lengths.shape, jnp.int32),
            pltpu.SMEM((balance.shape[0] // RUN,), jnp.int32),
            pltpu.SemaphoreType.DMA((2,)),
        ],
        compiler_params=limit(balance.shape[0]),
    )(balance, doc_lengths, by_head, *blocks)


def rows_kernel(n_after, listed, heads, reach, balance_in, docs_in, q_own, g_own, *refs):
    refs = refs[n_after:]
    n_blocks = len(listed)
    blocks, (att_out, qg_out), scratch = refs[:n_blocks], refs[n_blocks : n_blocks + 2], refs[n_blocks + 2 :]
    kv_all, key_win, value_win, att_buf, grad_buf, out_sem, *lists = scratch
    me = lax.axis_index("ctx")
    both, width = min(block.shape[0] for block in blocks), blocks[0].shape[1]
    tok_rows = both // 2
    runs_here = tok_rows // RUN
    run_rows = RUN * heads

    copies = start_lists(balance_in, docs_in, lists)
    load_blocks(me, listed, blocks, kv_all)
    finish_lists(copies, lists)

    out_copies = []
    for r in range(runs_here):
        place_run, _ = run_window(me, lists, kv_all, key_win, value_win, r, reach, runs_here, tok_rows)
        here = slice(r * run_rows, (r + 1) * run_rows)
        q_rows = q_own[here, :]
        g_rows = g_own[here, :]
        raw, one_over = weights_of(lists[1], place_run, key_win[r], q_rows, reach, heads)
        attended = contract(value_win[r], raw.astype(jnp.bfloat16), 0, 0) * one_over
        att_buf[here, :] = attended.T.astype(jnp.bfloat16)
        _, grad_scores = score_gradients(raw, one_over, value_win[r], g_rows)
        query_part = contract(key_win[r], grad_scores, 0, 0) * (1.0 / math.sqrt(width))
        grad_buf[here, :] = query_part.T.astype(jnp.bfloat16)
        for i, (source, out) in enumerate(((att_buf, att_out), (grad_buf, qg_out))):
            at = pl.ds(r * run_rows, run_rows)
            out_copies.append(pltpu.make_async_copy(source.at[at], out.at[at], out_sem.at[2 * r + i]))
            out_copies[-1].start()
    for copy in out_copies:
        copy.wait()


def query_side(balance, doc_lengths, own, after, blocks, heads, reach):
    listed, blocks = zip(*blocks)
    n_ctx = sum(len(ks) for ks in listed)
    both, width = min(block.shape[0] for block in blocks), blocks[0].shape[1]
    tok_rows = both // 2
    runs_here = tok_rows // RUN
    rows = own[0].shape[0]
    return pl.pallas_call(
        functools.partial(rows_kernel, len(after), listed, heads, reach),
        out_shape=[jax.ShapeDtypeStruct((rows, width), jnp.bfloat16)] * 2,
        in_specs=[ANY, ANY, VMEM, VMEM] + [ANY] * len(after) + [VMEM] * len(blocks),
        out_specs=[HBM] * 2,
        scratch_shapes=[
            pltpu.VMEM((n_ctx * both, width), jnp.bfloat16),
            pltpu.VMEM((runs_here, reach * RUN, width), jnp.bfloat16),
            pltpu.VMEM((runs_here, reach * RUN, width), jnp.bfloat16),
            pltpu.VMEM((rows, width), jnp.bfloat16),
            pltpu.VMEM((rows, width), jnp.bfloat16),
            pltpu.SemaphoreType.DMA((2 * runs_here,)),
            pltpu.SMEM(balance.shape, jnp.int32),
            pltpu.SMEM(doc_lengths.shape, jnp.int32),
            pltpu.SMEM((balance.shape[0] // RUN,), jnp.int32),
            pltpu.SemaphoreType.DMA((2,)),
        ],
        compiler_params=limit(balance.shape[0]),
    )(balance, doc_lengths, *own, *after, *blocks)


def body(n_ctx, n_head, queries, key_rows, value_rows, out_grad, doc_lengths, balance):
    tok_rows, heads, width = queries.shape
    seq_total = balance.shape[0]
    reach = seq_total // LONGEST_SHARE // RUN + 1

    def swap(array, k):
        return lax.ppermute(array, "ctx", [(i, i ^ k) for i in range(n_ctx)])

    own = [array.reshape(tok_rows * heads, width) for array in (queries, out_grad)]
    mine, balance, doc_lengths = pack(key_rows, value_rows, balance, doc_lengths)
    blocks = {0: mine}
    for k in (4, 1, 2, 3):
        if k not in MERGED:
            blocks[k] = swap(mine, k)
    other = [lax.ppermute(array, "head", [(i, n_head - 1 - i) for i in range(n_head)]) for array in own]
    merged = {}
    for k in FAR_ORDER:
        if k - 4 in MERGED:
            merged[k] = swap(join(mine, blocks[4], seq_total), k - 4)
        else:
            blocks[k] = swap(blocks[4], k - 4)
    blocks = [((k - 4, k), merged[k]) if k in merged else ((k,), blocks[k]) for k in BLOCK_ORDER if k not in MERGED]
    for bit, _ in high_bits(n_ctx):
        blocks += [(tuple(bit + k for k in ks), swap(block, bit)) for ks, block in blocks]
    terms = list(gradient_terms(balance, doc_lengths, order_heads(own, other, heads, seq_total), blocks, heads, reach))

    for bit, below in reversed(high_bits(n_ctx)):
        for k in below:
            terms[k] = terms[k] + swap(terms[bit + k].astype(jnp.bfloat16), bit).astype(jnp.float32)
    far = terms[4]
    for k in BACK_ORDER:
        far = far + swap(terms[k].astype(jnp.bfloat16), k - 4).astype(jnp.float32)
    far = far.astype(jnp.bfloat16)
    total = terms[0]
    for k in SUM_ORDER:
        term = far if k == 4 else terms[k].astype(jnp.bfloat16)
        total = total + swap(term, k).astype(jnp.float32)
    after = [far]
    attended, query_grad = query_side(balance, doc_lengths, own, after, blocks, heads, reach)
    combined = total.astype(jnp.bfloat16)
    return (
        attended.reshape(tok_rows, heads, width),
        query_grad.reshape(tok_rows, heads, width),
        combined[:tok_rows],
        combined[tok_rows:],
    )


def solution(mesh):
    return jax.shard_map(
        functools.partial(body, mesh.shape["ctx"], mesh.shape["head"]),
        mesh=mesh,
        in_specs=(
            P(("seq", "ctx"), "head", None),
            P(("seq", "ctx"), None),
            P(("seq", "ctx"), None),
            P(("seq", "ctx"), "head", None),
            P("seq"),
            P("seq"),
        ),
        out_specs=(
            P(("seq", "ctx"), "head", None),
            P(("seq", "ctx"), "head", None),
            P(("seq", "ctx"), None),
            P(("seq", "ctx"), None),
        ),
        check_vma=False,
    )
```
